512 devices in a mesh: ctx: 16 (over y, core), head: 4 (over x), seq: 8 (over z).
Axes of the slice: x: 4, y: 8, z: 8, core: 2. Of those that a mesh axis runs over, the one named last changes fastest.
Arguments:
- queries: bfloat16 [512, 128, 576], P('seq', 'head'), may hold values from -25 to 25
- latent_cache: bfloat16 [16384, 576], P('ctx'), may hold values from -12 to 12
- selected: int32 [512, 16, 384], P('seq', 'ctx'), may hold values from 0 to 1023, as said below
- counts: int32 [512, 16], P('seq', 'ctx'), may hold values from 1 to 384, 2048 in all within a row
- value_up: bfloat16 [4, 32, 512, 128], P('head', 'ctx'), may hold values from -0.25 to 0.25
- output_proj_weight: bfloat16 [4, 32, 128, 7168], P('head', 'ctx', None, 'seq'), may hold values from -0.046875 to 0.046875
Outputs:
- output: bfloat16 [512, 7168], P('seq', ('ctx', 'head'))
The draws below stay inside these ranges and needn't reach their ends.
Inputs may be any that keep to these rules, and one draw needn't show every extreme that they name: In each row selected[q,s,:] all entries are distinct; the first counts[q,s] of them are the selected tokens, later entries are ignored. Each row of counts sums to 2048; its largest entry is exactly 384.
All inputs are finite; a program needn't handle non-finite values. No bound on the sum of `counts` on one device may be relied on, other than what follows from the above.
Results may differ from the reference program's by a relative error of at most 0.006.
Values may be sent and summed in bfloat16 or wider, within the bound.
A program may use at most 64 MiB of HBM per device.

```python
import math
import jax
import jax.numpy as jnp
import numpy as np
from jax import lax

H = 128
LAT = 512
ROPE = 64
VDIM = 128
DMODEL = 7168
TOPK = 2048
CTX_DEV = 1024
HEADS_DEV = 32
MOST = 384
QTOK = 512
CTX = 16384
N_CTX = 16
N_HEAD = 4


def draw_queries(key, part):
    key = jax.random.fold_in(key, 1)
    first_key = jax.random.fold_in(key, 0)
    base = 0.25 * jnp.clip(jax.random.normal(first_key, (QTOK, H, LAT + ROPE), jnp.float32), -4.0, 4.0)
    return base.astype(jnp.bfloat16)


def draw_latent_cache(key, part):
    key = jax.random.fold_in(key, 2)
    first_key = jax.random.fold_in(key, 0)
    base = 2.0 * jnp.clip(jax.random.normal(first_key, (CTX, LAT + ROPE), jnp.float32), -4.0, 4.0)
    return base.astype(jnp.bfloat16)


def draw_selected(key, part):
    key = jax.random.fold_in(key, 3)
    raw = jax.random.randint(key, (QTOK, N_CTX, CTX_DEV), 0, 2 ** 30 // CTX_DEV)
    sorted_order = raw * CTX_DEV + jnp.arange(CTX_DEV, dtype=jnp.int32)
    order = jnp.argsort(sorted_order, axis=-1, stable=True)
    return order[:, :, :MOST].astype(jnp.int32)


def levels(rng, shape, pieces, low, high):
    factor_of = 1.0
    for dim, parts in pieces:
        heights = jax.random.uniform(jax.random.fold_in(jax.random.fold_in(rng, 6), dim), (parts,), jnp.float32, low / len(pieces), high / len(pieces))
        factor_of = factor_of * jnp.repeat(jnp.exp(heights), shape[dim] // parts).reshape((-1,) + (1,) * (len(shape) - 1 - dim))
    return factor_of


def profile(count, total, reach, skew):
    loads = [(1 << 20) // math.isqrt(grade ** skew) + 1 for grade in range(2, count + 1)]
    rest, given = total - reach - (count - 1), [1] * (count - 1)
    while rest > 0:
        movable = [i for i in range(count - 1) if given[i] < reach]
        mass, left = sum([loads[i] for i in movable]), rest
        for i in movable:
            addition = min(reach - given[i], max(1, left * loads[i] // mass), rest)
            given[i] = given[i] + addition
            rest = rest - addition
    return np.array([reach] + given)


def uneven(own_key, count, total, bound, skew):
    if count == 2:
        one = jax.random.randint(own_key, (), max(1, total - bound), min(bound, total - 1) + 1)
        return jnp.stack([one, total - one])
    tallies = jnp.asarray(profile(count, total, bound, skew), jnp.int32)
    pairs = (count - 1) // 2
    donor, sink = tallies[1:1 + 2 * pairs:2], tallies[2:2 + 2 * pairs:2]
    room = jnp.minimum(donor - 1, bound - sink)
    moved = jax.random.randint(jax.random.fold_in(own_key, 1), (pairs,), 0, 1 << 20) % (room + 1)
    tallies = tallies.at[1:1 + 2 * pairs:2].set(donor - moved).at[2:2 + 2 * pairs:2].set(sink + moved)
    return tallies[jax.random.permutation(jax.random.fold_in(own_key, 2), count)]


def noise(own_key, extent, width, limit, pieces=(), kind=jnp.bfloat16):
    result = jax.random.normal(own_key, extent, jnp.float32) * width
    if len(pieces) > 0:
        result = levels(own_key, extent, pieces, -0.22, 0.18) * result
    return jnp.clip(result, min=-limit, max=limit).astype(kind)


def setup_inputs(seed: int = 0) -> dict:
    key_list = jax.random.split(jax.random.key(seed), 7)
    return {
        "queries": draw_queries(jax.random.fold_in(key_list[6], 71), 0),
        "latent_cache": draw_latent_cache(jax.random.fold_in(key_list[6], 71), 0),
        "selected": draw_selected(jax.random.fold_in(key_list[6], 71), 0),
        "counts": jax.vmap(lambda own: uneven(own, N_CTX, TOPK, MOST, 2))(jax.random.split(key_list[3], QTOK)).reshape((QTOK, N_CTX)).astype(jnp.int32),
        "value_up": noise(key_list[4], (N_HEAD, HEADS_DEV, LAT, VDIM), LAT ** -0.5, 0.25, ((0, 4), (1, 16))),
        "output_proj_weight": noise(key_list[5], (N_HEAD, HEADS_DEV, VDIM, DMODEL), (H * VDIM) ** -0.5, 0.046875, ((0, 4), (1, 16), (3, 8))),
    }


softmax_scale = (0.1 * math.log(40.0) + 1.0) ** 2 / math.sqrt(192.0)

def shard_partial(query_rows, key_rows, count_here):
    scores = jnp.einsum('hd,kd->hk', query_rows.astype(jnp.float32), key_rows.astype(jnp.float32)) * softmax_scale
    slot_ids = jnp.arange(key_rows.shape[0], dtype=jnp.int32)
    scores = jnp.where((slot_ids < count_here)[None, :], scores, -jnp.inf)
    peak_score = lax.optimization_barrier(jnp.max(scores, axis=1, keepdims=True))
    weights = jnp.exp(scores - peak_score)
    totals = lax.optimization_barrier(jnp.sum(weights, axis=1, keepdims=True))
    weighted = jnp.dot(weights.astype(jnp.bfloat16), key_rows[:, :LAT], preferred_element_type=jnp.float32)
    return (weighted / totals, (peak_score + jnp.log(totals))[:, 0])

def reference(queries, latent_cache, selected, counts, value_up, output_proj_weight):

    def one_query(packed):
        query_rows, slot_rows, count_row = packed
        offsets = jnp.arange(N_CTX, dtype=jnp.int32) * CTX_DEV
        positions = (slot_rows + offsets[:, None]).astype(jnp.int32)
        key_rows = latent_cache[positions]
        part_out, part_lse = jax.vmap(shard_partial, in_axes=(None, 0, 0))(query_rows, key_rows, count_row)
        peak_score = lax.optimization_barrier(jnp.max(part_lse, axis=0))
        factor = jnp.exp(part_lse - peak_score)
        norm_sum = lax.optimization_barrier(jnp.sum(factor, axis=0))
        merged = lax.optimization_barrier(jnp.sum(factor[:, :, None] * part_out, axis=0)) / norm_sum[:, None]
        return merged.astype(jnp.bfloat16)
    merged = lax.map(one_query, (queries, selected, counts))
    head_up = value_up.reshape(H, LAT, VDIM)
    values = jnp.einsum('qhl,hlv->qhv', merged.astype(jnp.float32), head_up.astype(jnp.float32)).astype(jnp.bfloat16)
    flat = values.reshape(QTOK, H * VDIM)
    return jnp.dot(flat, output_proj_weight.reshape(H * VDIM, DMODEL), preferred_element_type=jnp.float32).astype(jnp.bfloat16)
```

```python
import functools
import math

import jax
import jax.numpy as jnp
from jax import lax
from jax.experimental import pallas as pl
from jax.experimental.pallas import tpu as pltpu
from jax.sharding import PartitionSpec as P

LAT = 512
VDIM = 128
LANES = 128
FAR = 1e30
MESH = pl.DeviceIdType.MESH
NY = 8
NZ = 8
NX = 4
Q = 64
BLOCK = 112
F32 = jnp.float32
BF16 = jnp.bfloat16

softmax_scale = (0.1 * math.log(40.0) + 1.0) ** 2 / math.sqrt(192.0)
exp2_scale = softmax_scale / math.log(2.0)


def dot_t(a, b):
    return lax.dot_general(a, b, (((1,), (1,)), ((), ())), preferred_element_type=F32)


def enter(peers):
    barrier = pltpu.get_barrier_semaphore()
    for peer in peers:
        pl.semaphore_signal(barrier, inc=1, device_id=peer, device_id_type=MESH)
    return barrier


def across(y, core):
    return lax.rem(y + NY, NY) * 2 + core


def attend_kernel(
    sel_ref, cnt_ref, q_ref, kv_ref, up_ref, out_ref,
    kv_buf, bias, q_own, s_buf, p_buf, part, lse, data_out, data_in, stat_out, stat_in,
    local_sem, pair_send, pair_recv, send_sem, recv_sem, stat_send, stat_recv,
):
    tokens, width = kv_ref.shape
    heads = q_ref.shape[1]
    slots = sel_ref.shape[1]
    tiles = tokens // LANES
    ctx = lax.axis_index("ctx")
    y, core = ctx // 2, lax.rem(ctx, 2)
    partner = {"ctx": y * 2 + 1 - core}
    sides = ({"ctx": across(y + 1, core)}, {"ctx": across(y - 1, core)})

    barrier = enter((partner,) + sides)
    own_kv = pltpu.make_async_copy(kv_ref, kv_buf.at[0], local_sem)
    own_kv.start()

    slot = lax.broadcasted_iota(jnp.int32, (1, slots), 1)
    tile_id = lax.broadcasted_iota(jnp.int32, (tiles, slots), 0)
    lane_id = lax.broadcasted_iota(jnp.int32, (LANES, slots), 0)

    pl.semaphore_wait(barrier, 3)
    pair_kv = pltpu.make_async_remote_copy(
        src_ref=kv_ref, dst_ref=kv_buf.at[1], send_sem=pair_send.at[0], recv_sem=pair_recv.at[0],
        device_id=partner, device_id_type=MESH,
    )
    pair_kv.start()

    def masks(g, carry):
        base = pl.multiple_of(g * 8, 8)
        sel = sel_ref[pl.ds(base, 8), :]
        cnt = cnt_ref[pl.ds(base, 8), :]
        fars = []
        for i in range(8):
            chosen = sel[i : i + 1, :]
            high = jnp.where(slot < cnt[i : i + 1, :], chosen >> 7, tiles)
            low = chosen & (LANES - 1)
            high_hot = (tile_id == high).astype(F32).astype(BF16)
            low_hot = (lane_id == low).astype(F32).astype(BF16)
            fars.append((dot_t(high_hot, low_hot) - 1.0) * FAR)
        for t in range(tiles):
            bias[0, pl.ds(base, 8), t * LANES : (t + 1) * LANES] = jnp.concatenate(
                [far[t : t + 1, :] for far in fars], axis=0
            )
        return carry

    lax.fori_loop(0, Q // 8, masks, 0)
    pair_bias = pltpu.make_async_remote_copy(
        src_ref=bias.at[0], dst_ref=bias.at[1], send_sem=pair_send.at[1], recv_sem=pair_recv.at[1],
        device_id=partner, device_id_type=MESH,
    )
    pair_bias.start()

    rows = lax.broadcasted_iota(jnp.int32, (256, 512), 0)
    cols = lax.broadcasted_iota(jnp.int32, (256, 512), 1)
    head = rows // 16
    wanted = (rows % 16) * heads + (head // 2) * 4 + core * 2 + head % 2
    pick = (cols == wanted).astype(F32).astype(BF16)
    for g in range(Q // 16):
        block = q_ref[g * 16 : (g + 1) * 16].reshape(512, width)
        own = jnp.dot(pick, block, preferred_element_type=F32).astype(BF16)
        q_own[:, g * 16 : (g + 1) * 16, :] = own.reshape(16, 16, width)

    own_kv.wait()
    pair_kv.wait()
    pair_bias.wait()

    def compute(unit, dests):
        for n, dest in enumerate(dests):
            q = q_own[pl.ds(dest * 2, 2)].reshape(128, width)
            for half in range(2):
                s_buf[n * 128 : (n + 1) * 128, half * tokens : (half + 1) * tokens] = dot_t(
                    q, kv_buf[half]
                )
        count = len(dests) * 128
        for r in range(0, count, 16):
            n, e, qs = r // 128, (r % 128) // 64, r % 64
            parts = []
            for half in range(2):
                for t in range(tiles):
                    a, b = half * tokens + t * LANES, t * LANES
                    parts.append(
                        s_buf[r : r + 16, a : a + LANES] + bias[half, qs : qs + 16, b : b + LANES]
                    )
            top = jnp.max(functools.reduce(jnp.maximum, parts), axis=1, keepdims=True)
            weights = [jnp.exp2((x - top) * exp2_scale) for x in parts]
            total = jnp.sum(functools.reduce(jnp.add, weights), axis=1, keepdims=True)
            for t, w in enumerate(weights):
                p_buf[r : r + 16, t * LANES : (t + 1) * LANES] = w.astype(BF16)
            value = top * softmax_scale + jnp.log(total)
            lse[n, e, qs : qs + 16, :] = jnp.broadcast_to(value, (16, LANES))
            part[n, e, qs : qs + 16, 0:LANES] = jnp.broadcast_to(1.0 / total, (16, LANES))
        for n in range(len(dests)):
            p = p_buf[n * 128 : (n + 1) * 128, :]
            o = jnp.dot(p[:, :tokens], kv_buf[0, :, :LAT], preferred_element_type=F32)
            o = o + jnp.dot(p[:, tokens:], kv_buf[1, :, :LAT], preferred_element_type=F32)
            for e in range(2):
                inv = part[n, e, :, 0:LANES]
                for t in range(LAT // LANES):
                    c = slice(t * LANES, (t + 1) * LANES)
                    part[n, e, :, c] = o[e * 64 : (e + 1) * 64, c] * inv

    def copies(side, u):
        return (
            pltpu.make_async_remote_copy(
                src_ref=data_out.at[side, u], dst_ref=data_in.at[side, u],
                send_sem=send_sem.at[side, u], recv_sem=recv_sem.at[side, u],
                device_id=sides[side], device_id_type=MESH,
            ),
            pltpu.make_async_remote_copy(
                src_ref=stat_out.at[side, u], dst_ref=stat_in.at[side, u],
                send_sem=stat_send.at[side, u], recv_sem=stat_recv.at[side, u],
                device_id=sides[side], device_id_type=MESH,
            ),
        )

    def send(side, u, values, level):
        for t in range(LAT // LANES):
            data_out[side, u, :, t * LANES : (t + 1) * LANES] = values[t].astype(BF16)
        stat_out[side, u] = jnp.concatenate([level, level], axis=0).T[0:8, :]
        for copy in copies(side, u):
            copy.start()

    def held(n, e):
        return [part[n, e, :, t * LANES : (t + 1) * LANES] for t in range(LAT // LANES)], lse[n, e]

    def merge(side, u, values, level):
        for copy in copies(side, u):
            copy.wait_recv()
        other = jnp.broadcast_to(stat_in[side, u, 0:1, :], (LANES, LANES)).T[0:64, :]
        top = jnp.maximum(other, level)
        w_in, w_own = jnp.exp(other - top), jnp.exp(level - top)
        total = w_in + w_own
        inv = 1.0 / total
        w_in, w_own = w_in * inv, w_own * inv
        mixed = [
            data_in[side, u, :, t * LANES : (t + 1) * LANES].astype(F32) * w_in + values[t] * w_own
            for t in range(LAT // LANES)
        ]
        return mixed, top + jnp.log(total)

    def dest(k):
        return lax.rem(y + k + NY, NY)

    compute(0, [dest(4)])
    for side in range(2):
        send(side, 0, *held(0, side))
    for hop in range(1, 4):
        compute(hop, [dest(4 - hop), dest(hop - 4)])
        base = 1 + 2 * (hop - 1)
        for order in range(2):
            for side in range(2):
                if hop == 1:
                    e = 1 - side if order == 0 else side
                    mine = held(side, e)
                    if order == 1:
                        mine = merge(side, 0, *mine)
                else:
                    e = 1 - side if order == 0 else side
                    mine = merge(side, base - 2 + e, *held(side, e))
                send(side, base + e, *mine)
    compute(4, [y])
    for e in range(2):
        mine = held(0, e)
        for side in range(2):
            mine = merge(side, 5 + e, *mine)
        merged = jnp.concatenate([m.astype(BF16) for m in mine[0]], axis=1)
        value = jnp.dot(merged, up_ref[e], preferred_element_type=F32)
        out_ref[:, e * VDIM : (e + 1) * VDIM] = value.astype(BF16)
    for side in range(2):
        for u in range(7):
            for copy in copies(side, u):
                copy.wait_send()


def attend(queries, latent_cache, selected, counts, value_up):
    rows, heads, width = queries.shape
    tokens = latent_cache.shape[0]
    vmem = pl.BlockSpec(memory_space=pltpu.VMEM)
    dma = pltpu.SemaphoreType.DMA
    return pl.pallas_call(
        attend_kernel,
        out_shape=jax.ShapeDtypeStruct((rows, 2 * VDIM), BF16),
        in_specs=[vmem, vmem, vmem, pl.BlockSpec(memory_space=pl.ANY), vmem],
        out_specs=vmem,
        scratch_shapes=[
            pltpu.VMEM((2, tokens, width), BF16),
            pltpu.VMEM((2, rows, tokens), F32),
            pltpu.VMEM((16, rows, width), BF16),
            pltpu.VMEM((256, 2 * tokens), F32),
            pltpu.VMEM((256, 2 * tokens), BF16),
            pltpu.VMEM((2, 2, rows, LAT), F32),
            pltpu.VMEM((2, 2, rows, LANES), F32),
            pltpu.VMEM((2, 7, rows, LAT), BF16),
            pltpu.VMEM((2, 7, rows, LAT), BF16),
            pltpu.VMEM((2, 7, 8, LANES), F32),
            pltpu.VMEM((2, 7, 8, LANES), F32),
            dma, dma((2,)), dma((2,)), dma((2, 7)), dma((2, 7)), dma((2, 7)), dma((2, 7)),
        ],
        compiler_params=pltpu.CompilerParams(
            collective_id=0, has_side_effects=True, vmem_limit_bytes=48 * 1024 * 1024
        ),
    )(selected, counts, queries, latent_cache, value_up)


def project_kernel(
    val_ref, w_ref, out_ref,
    vals, w_own, w_pair, own_x, x_out, x_in, z_out, z_in, y_in,
    w_send, w_recv, z_send, z_recv, c_send, c_recv, x_send, x_recv, a_send, a_recv, y_send, y_recv,
):
    ctx, x, z = lax.axis_index("ctx"), lax.axis_index("head"), lax.axis_index("seq")
    y, core = ctx // 2, lax.rem(ctx, 2)
    partner = {"ctx": y * 2 + 1 - core}

    def at_y(k):
        return {"ctx": across(y + k, core)}

    def at_x(k):
        return {"head": lax.rem(x + k + NX, NX)}

    def at_z(k):
        return {"seq": lax.rem(z + k + NZ, NZ)}

    barrier = enter(
        [partner]
        + [at_y(k) for k in range(1, NY)]
        + [at_x(k) for k in range(1, NX)]
        + [at_z(k) for k in range(1, NZ)]
    )
    rows = w_ref.shape[0]
    pad = jnp.zeros((rows, LANES - BLOCK), BF16)
    for k in range(NX):
        low = w_ref[:, k * BLOCK : (k + 1) * BLOCK]
        high = w_ref[:, (NX + k) * BLOCK : (NX + k + 1) * BLOCK]
        c = slice(k * LANES, (k + 1) * LANES)
        low = jnp.concatenate([low, pad], axis=1)
        high = jnp.concatenate([high, pad], axis=1)
        w_own[0, :, c] = jnp.where(core == 0, low, high)
        w_pair[:, c] = jnp.where(core == 0, high, low)
    vals[0, z] = val_ref[...]
    pl.semaphore_wait(barrier, 1 + (NY - 1) + (NX - 1) + (NZ - 1))

    def remote(src, dst, s, r, peer):
        return pltpu.make_async_remote_copy(
            src_ref=src, dst_ref=dst, send_sem=s, recv_sem=r, device_id=peer, device_id_type=MESH
        )

    order = [0, 1, 7, 2, 6, 3, 5, 4]
    gather = {
        d: remote(vals.at[0, z], vals.at[0, z], z_send.at[d], z_recv.at[d], at_z(d))
        for d in order[1:]
    }
    for d in order[1:]:
        gather[d].start()
    w_copy = remote(w_pair, w_own.at[1], w_send, w_recv, partner)
    w_copy.start()

    forward = {}
    for d in order:
        j = lax.rem(z - d + NZ, NZ)
        if d:
            arrival = remote(vals.at[0, j], vals.at[0, j], z_send.at[d], z_recv.at[d], at_z(d))
            arrival.wait_recv()
        forward[d] = remote(vals.at[0, j], vals.at[1, j], c_send.at[d], c_recv.at[d], partner)
        forward[d].start()
    w_copy.wait()

    cross = {}
    for d in order:
        j = lax.rem(z - d + NZ, NZ)
        forward[d].wait_recv()
        terms = jnp.dot(vals[0, j], w_own[0], preferred_element_type=F32)
        terms = terms + jnp.dot(vals[1, j], w_own[1], preferred_element_type=F32)
        for k in range(NX):
            x_out[d, k] = terms[:, k * LANES : (k + 1) * LANES]
        own_x[d] = x_out[d, x]
        for k in range(1, NX):
            peer = lax.rem(x + k, NX)
            z_out[d, k] = x_out[d, peer].astype(BF16)
            cross[d, k] = remote(
                z_out.at[d, k], x_in.at[d, k], x_send.at[d, k], x_recv.at[d, k], at_x(k)
            )
            cross[d, k].start()

    spread = {}
    for d in order:
        total = own_x[d]
        for k in range(1, NX):
            cross[d, k].wait_recv()
            total = total + x_in[d, k].astype(F32)
        if d == 0:
            z_in[z] = total.astype(BF16)
        else:
            z_out[d, 0] = total.astype(BF16)
            spread[d] = remote(z_out.at[d, 0], z_in.at[z], a_send.at[d], a_recv.at[d], at_z(-d))
            spread[d].start()
    for d in order[1:]:
        spread[d].wait_recv()

    last = {}
    for k in [1, 7, 2, 6, 3, 5, 4]:
        target = lax.rem(y + k, NY)
        last[k] = remote(z_in.at[target], y_in.at[k], y_send.at[k], y_recv.at[k], at_y(k))
        last[k].start()
    total = z_in[y].astype(F32)
    for k in [1, 7, 2, 6, 3, 5, 4]:
        last[k].wait_recv()
        total = total + y_in[k].astype(F32)
    out_ref[...] = total[:, :BLOCK].astype(BF16)
    for d in order:
        if d:
            gather[d].wait_send()
            spread[d].wait_send()
        forward[d].wait_send()
        for k in range(1, NX):
            cross[d, k].wait_send()
    for k in range(1, NY):
        last[k].wait_send()


def project(values, weight):
    rows = values.shape[0]
    vmem = pl.BlockSpec(memory_space=pltpu.VMEM)
    dma = pltpu.SemaphoreType.DMA
    return pl.pallas_call(
        project_kernel,
        out_shape=jax.ShapeDtypeStruct((rows, BLOCK), BF16),
        in_specs=[vmem, vmem],
        out_specs=vmem,
        scratch_shapes=[
            pltpu.VMEM((2, NZ, rows, 2 * VDIM), BF16),
            pltpu.VMEM((2, 2 * VDIM, NX * LANES), BF16),
            pltpu.VMEM((2 * VDIM, NX * LANES), BF16),
            pltpu.VMEM((NZ, rows, LANES), F32),
            pltpu.VMEM((NZ, NX, rows, LANES), F32),
            pltpu.VMEM((NZ, NX, rows, LANES), BF16),
            pltpu.VMEM((NZ, NX, rows, LANES), BF16),
            pltpu.VMEM((NZ, rows, LANES), BF16),
            pltpu.VMEM((NY, rows, LANES), BF16),
            dma, dma, dma((NZ,)), dma((NZ,)), dma((NZ,)), dma((NZ,)), dma((NZ, NX)), dma((NZ, NX)),
            dma((NZ,)), dma((NZ,)), dma((NY,)), dma((NY,)),
        ],
        compiler_params=pltpu.CompilerParams(
            collective_id=1, has_side_effects=True, vmem_limit_bytes=32 * 1024 * 1024
        ),
    )(values, weight)


def shards(queries, latent_cache, selected, counts, value_up, output_proj_weight):
    weight = output_proj_weight[0].reshape(2 * VDIM, output_proj_weight.shape[3])
    values = attend(queries, latent_cache, selected[:, 0, :], counts, value_up[0])
    return project(values, weight)


def solution(mesh):
    in_specs = (
        P("seq", "head", None),
        P("ctx", None),
        P("seq", "ctx", None),
        P("seq", "ctx"),
        P("head", "ctx", None, None),
        P("head", "ctx", None, "seq"),
    )
    out_specs = P("seq", ("ctx", "head"))
    return jax.shard_map(shards, mesh=mesh, in_specs=in_specs, out_specs=out_specs, check_vma=False)
```

```python
import functools
import math

import jax
import jax.numpy as jnp
from jax import lax
from jax.experimental import pallas as pl
from jax.experimental.pallas import tpu as pltpu
from jax.sharding import PartitionSpec as P

LAT = 512
VDIM = 128
LANES = 128
FAR = 1e30
MESH = pl.DeviceIdType.MESH
NY = 8
NZ = 8
NX = 4
Q = 64
BLOCK = 112
F32 = jnp.float32
BF16 = jnp.bfloat16

softmax_scale = (0.1 * math.log(40.0) + 1.0) ** 2 / math.sqrt(192.0)
exp2_scale = softmax_scale / math.log(2.0)


def iota(shape, axis):
    return lax.broadcasted_iota(jnp.int32, shape, axis)


def dot(a, b):
    return jnp.dot(a, b, preferred_element_type=F32)


def remote(src, dst, s, r, peer):
    return pltpu.make_async_remote_copy(
        src_ref=src, dst_ref=dst, send_sem=s, recv_sem=r, device_id=peer, device_id_type=MESH
    )


def lane_tiles(width):
    return [slice(t * LANES, (t + 1) * LANES) for t in range(width // LANES)]


def build_bias(sel_v, cnt_v, words, bias):
    tokens = bias.shape[1]
    lane = iota((1, LANES), 1)
    s = sel_v[...].reshape(Q, 384).astype(F32)
    first = jnp.concatenate([s[:, 0:128], s[:, 128:256]], axis=0).T
    last = jnp.concatenate([s[:, 256:384], s[:, 256:384]], axis=0).T
    last = jnp.where(lane < 64, last[0:64], last[64:128])
    sel_t = jnp.concatenate([first, last], axis=0).astype(jnp.int32)
    row = iota((192, LANES), 0)
    late = (iota((192, LANES), 1) >= 64).astype(jnp.int32)
    slot = jnp.where(row < 128, row + 128 * late, row + 128 + 64 * late)
    cnt = cnt_v[...]
    cnt = jnp.concatenate([cnt, cnt], axis=1)
    high = sel_t >> 4
    value = jnp.where(slot < cnt, (1 << (sel_t & 15)).astype(F32), 0.0)
    for k in range(64):
        words[k : k + 1, :] = jnp.sum(jnp.where(high == k, value, 0.0), axis=0, keepdims=True)
    w = words[...]
    w = (w + pltpu.roll(w, 64, 1)).astype(jnp.int32)
    bytes_t = jnp.concatenate([(w & 255).astype(F32), (w >> 8).astype(F32)], axis=0).T
    token = iota((128, tokens), 1)
    place = ((token >> 3) & 1) * 64 + (token >> 4)
    expand = (place == iota((128, tokens), 0)).astype(F32).astype(BF16)
    found = dot(bytes_t[0:Q].astype(BF16), expand).astype(jnp.int32)
    bit = (found >> (iota((Q, tokens), 1) & 7)) & 1
    bias[...] = jnp.where(bit == 1, 0.0, -FAR)


def kernel(
    sel_ref, cnt_ref, q_ref, kvt_ref, up_ref, w_ref, out_ref,
    sel_v, cnt_v, q_v, kvt_v, up_v, w_v, local_sem,
    words, bias, kv_v, q_t, s_buf, p_buf, inv_buf,
    part, lse, pair_in, pair_lse, pair_send, pair_recv, own, own_lse,
    data_out, data_in, stat_out, stat_in, ring_send, ring_recv,
    val_v, vals, w_all, w_send, w_recv, twin_send, twin_recv, z_send, z_recv,
    x_f, x_out, x_in, x_send, x_recv, z_out, z_in, a_send, a_recv, y_in, y_send, y_recv,
):
    width = kvt_ref.shape[0]
    ctx, x, z = lax.axis_index("ctx"), lax.axis_index("head"), lax.axis_index("seq")
    y, core = ctx // 2, lax.rem(ctx, 2)
    partner = {"ctx": y * 2 + 1 - core}

    def at_y(k):
        return {"ctx": lax.rem(y + k + NY, NY) * 2 + core}

    def at_z(k, c):
        return {"ctx": y * 2 + c, "seq": lax.rem(z + k + NZ, NZ)}

    def at_x(k):
        return {"head": lax.rem(x + k, NX)}

    def fetch(i, src, dst):
        copy = pltpu.make_async_copy(src, dst, local_sem.at[i])
        copy.start()
        return copy

    fetch_sel = fetch(0, sel_ref, sel_v)
    fetch_cnt = fetch(1, cnt_ref, cnt_v)
    fetch_kvt = fetch(2, kvt_ref, kvt_v)
    first_half = lax.rem(y + 4, NY) // 4
    halves = (first_half, 1 - first_half)
    fetch_q = [
        fetch(3 + i, q_ref.at[:, pl.ds(pl.multiple_of(half * 16, 16), 16), :], q_v.at[i])
        for i, half in enumerate(halves)
    ]
    fetch_up = fetch(5, up_ref, up_v)
    fetch_w = fetch(6, w_ref, w_v.at[0])

    barrier = pltpu.get_barrier_semaphore()
    peers = [partner] + [at_y(k) for k in range(1, NY)] + [at_x(k) for k in range(1, NX)]
    peers += [at_z(k, c) for k in range(1, NZ) for c in range(2)]
    for peer in peers:
        pl.semaphore_signal(barrier, inc=1, device_id=peer, device_id_type=MESH)

    fetch_sel.wait()
    fetch_cnt.wait()
    build_bias(sel_v, cnt_v, words, bias)
    fetch_kvt.wait()
    kv_v[...] = kvt_v[0:LAT, :].T
    r, c = iota((256, 256), 0), iota((256, 256), 1)
    swap = (c == (r & 15) * 16 + (r >> 4)).astype(F32).astype(BF16)

    def by_head(i):
        fetch_q[i].wait()
        for g in range(Q // 16):
            block = q_v[i, g * 16 : (g + 1) * 16].reshape(256, width)
            q_t[pl.ds(halves[i] * 16, 16), g * 16 : (g + 1) * 16, :] = (
                dot(swap, block).astype(BF16).reshape(16, 16, width)
            )

    by_head(0)

    def dest(u, n):
        return lax.rem(y + (4 - u if n == 0 else u - 4) + NY, NY)

    sequence = ((0, 0), (1, 0), (1, 1), (2, 0), (2, 1), (3, 0), (3, 1), (4, 0))

    def score(i):
        q = q_t[pl.ds(dest(*sequence[i]) * 4, 4)].reshape(256, width)
        s_buf[i % 2] = dot(q, kvt_v[...])

    def compute(i):
        if 0 < i < len(sequence) - 1:
            score(i + 1)
        (u, n), m = sequence[i], i % 2
        for r in range(0, 256, 16):
            h, qs = r // 64, r % 64
            parts = [s_buf[m, r : r + 16, t] + bias[qs : qs + 16, t] for t in lane_tiles(1024)]
            top = jnp.max(functools.reduce(jnp.maximum, parts), axis=1, keepdims=True)
            weights = [jnp.exp2((part - top) * exp2_scale) for part in parts]
            total = jnp.sum(functools.reduce(jnp.add, weights), axis=1, keepdims=True)
            for t, value in zip(lane_tiles(1024), weights):
                p_buf[m, r : r + 16, t] = value.astype(BF16)
            level = top * softmax_scale + jnp.log(total)
            lse[u, n, h, qs : qs + 16, :] = jnp.broadcast_to(level, (16, LANES))
            inv_buf[m, r : r + 16, :] = jnp.broadcast_to(1.0 / total, (16, LANES))
        o = dot(p_buf[m], kv_v[...])
        for h in range(4):
            inv = inv_buf[m, h * 64 : (h + 1) * 64, :]
            for t in lane_tiles(LAT):
                part[u, n, h, :, t] = o[h * 64 : (h + 1) * 64, t] * inv

    def pair(u, n):
        theirs = pl.ds(2 * (1 - core), 2)
        return (
            remote(
                lse.at[u, n, theirs], pair_lse.at[u, n],
                pair_send.at[u, n, 0], pair_recv.at[u, n, 0], partner,
            ),
            remote(
                part.at[u, n, theirs], pair_in.at[u, n],
                pair_send.at[u, n, 1], pair_recv.at[u, n, 1], partner,
            ),
        )

    def pair_start(u, n):
        for copy in pair(u, n):
            copy.start()

    def pair_merge(u, n):
        for copy in pair(u, n):
            copy.wait_recv()
        for e in range(2):
            rows = slice(e * 64, (e + 1) * 64)
            mine, theirs = lse[u, n, 2 * core + e], pair_lse[u, n, e]
            top = jnp.maximum(mine, theirs)
            a, b = jnp.exp(mine - top), jnp.exp(theirs - top)
            total = a + b
            inv = 1.0 / total
            a, b = a * inv, b * inv
            for t in lane_tiles(LAT):
                own[u, n, rows, t] = part[u, n, 2 * core + e, :, t] * a + pair_in[u, n, e, :, t] * b
            own_lse[u, n, rows, :] = top + jnp.log(total)

    sides = (at_y(1), at_y(-1))

    def slot_of(hop, e):
        return 0 if hop == 0 else 2 * hop - 1 + e

    def link(side, i, k):
        out, into = ((stat_out, stat_in), (data_out, data_in))[k]
        return remote(
            out.at[side, i], into.at[side, i],
            ring_send.at[side, i, k], ring_recv.at[side, i, k], sides[side],
        )

    def incoming(side, i):
        link(side, i, 0).wait_recv()
        return jnp.broadcast_to(stat_in[side, i, 0:1, :], (LANES, LANES)).T[0:64, :]

    def mix(levels):
        top = functools.reduce(jnp.maximum, levels)
        scales = [jnp.exp(level - top) for level in levels]
        total = functools.reduce(jnp.add, scales)
        inv = 1.0 / total
        return [scale * inv for scale in scales], top + jnp.log(total)

    def send(side, hop, e):
        i, n = slot_of(hop, e), 0 if hop == 0 else side
        rows = slice(e * 64, (e + 1) * 64)
        fresh = hop == 0 or (hop == 1 and e != side)
        level = own_lse[hop, n, rows, :]
        if not fresh:
            j = slot_of(hop - 1, e)
            (a, b), level = mix([level, incoming(side, j)])
        stat_out[side, i] = jnp.concatenate([level, level], axis=0).T[0:8, :]
        link(side, i, 0).start()
        if fresh:
            data_out[side, i] = own[hop, n, rows, :].astype(BF16)
        else:
            link(side, j, 1).wait_recv()
            for t in lane_tiles(LAT):
                mixed = own[hop, n, rows, t] * a + data_in[side, j, :, t].astype(F32) * b
                data_out[side, i, :, t] = mixed.astype(BF16)
        link(side, i, 1).start()

    score(0)
    compute(0)
    pl.semaphore_wait(barrier, len(peers))
    pair_start(0, 0)
    twin = z + 1 - 2 * lax.rem(z, 2)
    w_twin = remote(w_ref, w_v.at[1], twin_send, twin_recv, {"seq": twin})
    w_twin.start()
    by_head(1)
    score(1)
    pair_merge(0, 0)
    send(0, 0, 0)
    send(1, 0, 1)
    compute(1)
    pair_start(1, 0)
    compute(2)
    pair_start(1, 1)
    pair_merge(1, 0)
    send(0, 1, 1)
    compute(3)
    pair_start(2, 0)
    pair_merge(1, 1)
    send(1, 1, 0)
    send(0, 1, 0)
    send(1, 1, 1)
    compute(4)
    pair_start(2, 1)
    pair_merge(2, 0)
    send(0, 2, 1)
    compute(5)
    pair_start(3, 0)
    pair_merge(2, 1)
    send(1, 2, 0)
    send(0, 2, 0)
    send(1, 2, 1)
    compute(6)
    pair_start(3, 1)
    pair_merge(3, 0)
    send(0, 3, 1)
    compute(7)
    pair_start(4, 0)
    pair_merge(3, 1)
    send(1, 3, 0)
    send(0, 3, 0)
    send(1, 3, 1)

    fetch_w.wait()
    fetch_up.wait()
    pad = jnp.zeros((w_v.shape[1], LANES - BLOCK), BF16)

    def w_copy(m, c):
        return remote(w_all.at[m, c], w_all.at[m, c], w_send.at[m], w_recv.at[m], partner)

    for m in range(2):
        if m == 1:
            w_twin.wait_recv()
        for k, t in enumerate(lane_tiles(8 * LANES)):
            columns = w_v[m, :, k * BLOCK : (k + 1) * BLOCK]
            w_all[m, core, :, t] = jnp.concatenate([columns, pad], axis=1)
        w_copy(m, core).start()

    pair_merge(4, 0)
    for e in (1, 0):
        rows, i = slice(e * 64, (e + 1) * 64), slot_of(3, e)
        (a, b, c), _ = mix([own_lse[4, 0, rows, :], incoming(0, i), incoming(1, i)])
        for side in range(2):
            link(side, i, 1).wait_recv()
        merged = jnp.concatenate(
            [
                own[4, 0, rows, t] * a
                + data_in[0, i, :, t].astype(F32) * b
                + data_in[1, i, :, t].astype(F32) * c
                for t in lane_tiles(LAT)
            ],
            axis=1,
        )
        upper = merged.astype(BF16)
        lower = (merged - upper.astype(F32)).astype(BF16)
        value = dot(upper, up_v[e]) + dot(lower, up_v[e])
        val_v[:, e * VDIM : (e + 1) * VDIM] = value.astype(BF16)

    odd = lax.rem(z, 2)
    step = 2 * odd - 1

    def at_target(i):
        return at_z((1, 1, -2, 3)[i] * step, i % 2)

    for i in (3, 2, 1):
        remote(
            val_v, vals.at[i, core], z_send.at[i], z_recv.at[i, core], at_target(i)
        ).start()
    at_pair = remote(val_v, vals.at[0, core], z_send.at[0], z_recv.at[0, core], partner)

    @pl.when(core == 1)
    def _():
        at_pair.start()

    @pl.when(core == 0)
    def _():
        vals[0, 0] = val_v[...]

    def block_of(i):
        return lax.rem(z + step * i + NZ, NZ)

    swap_order = (block_of(core + 2) < block_of(core)).astype(jnp.int32)

    def distance(p):
        return core + 2 * (swap_order if p < 2 else 1 - swap_order)

    def await_half(i, h):
        remote(val_v, vals.at[i, h], z_send.at[0], z_recv.at[i, h], partner).wait_recv()

    for m in range(2):
        w_copy(m, 1 - core).wait_recv()

    def cross(p, k):
        return remote(
            x_out.at[p, k], x_in.at[p, k], x_send.at[p, k], x_recv.at[p, k], at_x(k + 1)
        )

    for p in range(4):
        i, m = distance(p), p % 2
        if m == 0:

            @pl.when(i != 0)
            def _():
                await_half(i, 0)

            await_half(i, 1)
        terms = dot(vals[i, 0], w_all[m, 0]) + dot(vals[i, 1], w_all[m, 1])
        for k, t in enumerate(lane_tiles(8 * LANES)):
            x_f[p, k] = terms[:, t]
        for k in (0, 2, 1):
            to = lax.rem(x + k + 1, NX)
            for c in range(2):
                x_out[p, k, c] = x_f[p, c * NX + to].astype(BF16)
            cross(p, k).start()

    def spread(p, c):
        column = twin if p % 2 else z
        to = {"ctx": y * 2 + c, "seq": block_of(distance(p))}
        return remote(
            z_out.at[p, c], z_in.at[column], a_send.at[p, c], a_recv.at[column], to
        )

    for p in range(4):
        for k in (0, 2, 1):
            cross(p, k).wait_recv()
        for c in range(2):
            total = x_f[p, c * NX + x]
            for k in range(3):
                total = total + x_in[p, k, c].astype(F32)
            z_out[p, c] = total.astype(BF16)
            if c == 0:

                @pl.when(distance(p) == 0)
                def _():
                    z_in[twin if p % 2 else z] = z_out[p, 0]

                @pl.when(distance(p) != 0)
                def _():
                    spread(p, 0).start()

            else:
                spread(p, c).start()

    def last(k):
        to = lax.rem(y + k, NY)
        return remote(z_in.at[to], y_in.at[k], y_send.at[k], y_recv.at[k], at_y(k))

    for block in range(NZ):

        @pl.when(((block != z) & (block != twin)) | (core == 1))
        def _():
            remote(
                z_out.at[0, 0], z_in.at[block], a_send.at[0, 0], a_recv.at[block], partner
            ).wait_recv()

        k = lax.rem(block - y + NY, NY)

        @pl.when(k != 0)
        def _():
            last(k).start()

    total = z_in[y].astype(F32)
    for k in (1, 7, 2, 6, 3, 5, 4):
        last(k).wait_recv()
        total = total + y_in[k].astype(F32)
    out_ref[...] = total[:, :BLOCK].astype(BF16)

    for u in range(5):
        for n in range(1 if u in (0, 4) else 2):
            for copy in pair(u, n):
                copy.wait_send()
    for side in range(2):
        for i in range(7):
            for k in range(2):
                link(side, i, k).wait_send()
    w_twin.wait_send()
    for m in range(2):
        w_copy(m, core).wait_send()
    for i in range(1, 4):
        remote(val_v, vals.at[i, core], z_send.at[i], z_recv.at[i, core], partner).wait_send()

    @pl.when(core == 1)
    def _():
        at_pair.wait_send()

    for p in range(4):
        for k in range(3):
            cross(p, k).wait_send()
        spread(p, 1).wait_send()

        @pl.when(distance(p) != 0)
        def _():
            spread(p, 0).wait_send()

    for k in range(1, NY):
        last(k).wait_send()


def shards(queries, latent_cache, selected, counts, value_up, output_proj_weight):
    rows, heads, width = queries.shape
    tokens = latent_cache.shape[0]
    weight = output_proj_weight[0].reshape(2 * VDIM, output_proj_weight.shape[3])
    hbm = pl.BlockSpec(memory_space=pl.ANY)
    vmem, dma = pltpu.VMEM, pltpu.SemaphoreType.DMA
    return pl.pallas_call(
        kernel,
        out_shape=jax.ShapeDtypeStruct((rows, BLOCK), BF16),
        in_specs=[hbm] * 6,
        out_specs=pl.BlockSpec(memory_space=pltpu.VMEM),
        scratch_shapes=[
            vmem(selected.shape, jnp.int32),
            vmem((1, rows), jnp.int32),
            vmem((2, rows, 16, width), BF16),
            vmem((width, tokens), BF16),
            vmem((2, LAT, VDIM), BF16),
            vmem((2,) + weight.shape, BF16),
            dma((7,)),
            vmem((64, LANES), F32),
            vmem((rows, tokens), F32),
            vmem((tokens, LAT), BF16),
            vmem((heads, rows, width), BF16),
            vmem((2, 256, tokens), F32),
            vmem((2, 256, tokens), BF16),
            vmem((2, 256, LANES), F32),
            vmem((5, 2, 4, rows, LAT), F32),
            vmem((5, 2, 4, rows, LANES), F32),
            vmem((5, 2, 2, rows, LAT), F32),
            vmem((5, 2, 2, rows, LANES), F32),
            dma((5, 2, 2)),
            dma((5, 2, 2)),
            vmem((5, 2, 2 * rows, LAT), F32),
            vmem((5, 2, 2 * rows, LANES), F32),
            vmem((2, 7, rows, LAT), BF16),
            vmem((2, 7, rows, LAT), BF16),
            vmem((2, 7, 8, LANES), F32),
            vmem((2, 7, 8, LANES), F32),
            dma((2, 7, 2)),
            dma((2, 7, 2)),
            vmem((rows, 2 * VDIM), BF16),
            vmem((4, 2, rows, 2 * VDIM), BF16),
            vmem((2, 2, 2 * VDIM, 8 * LANES), BF16),
            dma((2,)),
            dma((2,)),
            dma,
            dma,
            dma((4,)),
            dma((4, 2)),
            vmem((4, 8, rows, LANES), F32),
            vmem((4, 3, 2, rows, LANES), BF16),
            vmem((4, 3, 2, rows, LANES), BF16),
            dma((4, 3)),
            dma((4, 3)),
            vmem((4, 2, rows, LANES), BF16),
            vmem((NZ, rows, LANES), BF16),
            dma((4, 2)),
            dma((NZ,)),
            vmem((NY, rows, LANES), BF16),
            dma((NY,)),
            dma((NY,)),
        ],
        compiler_params=pltpu.CompilerParams(
            collective_id=0, has_side_effects=True, vmem_limit_bytes=60 * 1024 * 1024
        ),
    )(selected, counts.T, queries, latent_cache.T, value_up[0], weight)


def solution(mesh):
    in_specs = (
        P("seq", "head", None),
        P("ctx", None),
        P("seq", "ctx", None),
        P("seq", "ctx"),
        P("head", "ctx", None, None),
        P("head", "ctx", None, "seq"),
    )
    out_specs = P("seq", ("ctx", "head"))
    return jax.shard_map(shards, mesh=mesh, in_specs=in_specs, out_specs=out_specs, check_vma=False)
```

```python
import functools
import math

import jax
import jax.numpy as jnp
from jax import lax
from jax.experimental import pallas as pl
from jax.experimental.pallas import tpu as pltpu
from jax.sharding import PartitionSpec as P

LAT = 512
VDIM = 128
LANES = 128
FAR = 1e30
MESH = pl.DeviceIdType.MESH
NY = 8
NZ = 8
NX = 4
Q = 64
BLOCK = 112
F32 = jnp.float32
BF16 = jnp.bfloat16

softmax_scale = (0.1 * math.log(40.0) + 1.0) ** 2 / math.sqrt(192.0)
exp2_scale = softmax_scale / math.log(2.0)


def iota(shape, axis):
    return lax.broadcasted_iota(jnp.int32, shape, axis)


def dot(a, b):
    return jnp.dot(a, b, preferred_element_type=F32)


def remote(src, dst, s, r, peer):
    return pltpu.make_async_remote_copy(
        src_ref=src, dst_ref=dst, send_sem=s, recv_sem=r, device_id=peer, device_id_type=MESH
    )


def lane_tiles(width):
    return [slice(t * LANES, (t + 1) * LANES) for t in range(width // LANES)]


def build_bias(sel_v, cnt_v, words, bias, between):
    tokens = bias.shape[1]
    lane = iota((1, LANES), 1)
    s = sel_v[...].reshape(Q, 384).astype(F32)
    first = jnp.concatenate([s[:, 0:128], s[:, 128:256]], axis=0).T
    last = jnp.concatenate([s[:, 256:384], s[:, 256:384]], axis=0).T
    last = jnp.where(lane < 64, last[0:64], last[64:128])
    sel_t = jnp.concatenate([first, last], axis=0).astype(jnp.int32)
    row = iota((192, LANES), 0)
    late = (iota((192, LANES), 1) >= 64).astype(jnp.int32)
    slot = jnp.where(row < 128, row + 128 * late, row + 128 + 64 * late)
    cnt = cnt_v[...]
    cnt = jnp.concatenate([cnt, cnt], axis=1)
    high = sel_t >> 4
    value = jnp.where(slot < cnt, (1 << (sel_t & 15)).astype(F32), 0.0)
    for k in range(64):
        words[k : k + 1, :] = jnp.sum(jnp.where(high == k, value, 0.0), axis=0, keepdims=True)
        between(k)
    w = words[...]
    w = (w + pltpu.roll(w, 64, 1)).astype(jnp.int32)
    bytes_t = jnp.concatenate([(w & 255).astype(F32), (w >> 8).astype(F32)], axis=0).T
    token = iota((128, tokens), 1)
    place = ((token >> 3) & 1) * 64 + (token >> 4)
    expand = (place == iota((128, tokens), 0)).astype(F32).astype(BF16)
    found = dot(bytes_t[0:Q].astype(BF16), expand).astype(jnp.int32)
    bit = (found >> (iota((Q, tokens), 1) & 7)) & 1
    bias[...] = jnp.where(bit == 1, 0.0, -FAR)


def kernel(
    sel_ref, cnt_ref, q_ref, kvt_ref, up_ref, w_ref, out_ref,
    sel_v, cnt_v, q_v, kvt_v, up_v, w_v, local_sem,
    words, bias, kv_v, q_t, s_buf, p_buf, inv_buf,
    part, pair_in, pair_send, pair_recv, own, own_lse,
    data_out, data_in, stat_out, stat_in, ring_send, ring_recv,
    val_v, vals, w_all, w_send, w_recv, twin_send, twin_recv, z_send, z_recv,
    x_f, x_out, x_in, x_send, x_recv, z_out, z_in, a_send, a_recv, y_in, y_send, y_recv,
):
    width = kvt_ref.shape[0]
    ctx, x, z = lax.axis_index("ctx"), lax.axis_index("head"), lax.axis_index("seq")
    y, core = ctx // 2, lax.rem(ctx, 2)
    partner = {"ctx": y * 2 + 1 - core}

    def at_y(k):
        return {"ctx": lax.rem(y + k + NY, NY) * 2 + core}

    def at_z(k, c):
        return {"ctx": y * 2 + c, "seq": lax.rem(z + k + NZ, NZ)}

    def at_x(k):
        return {"head": lax.rem(x + k, NX)}

    def fetch(i, src, dst):
        copy = pltpu.make_async_copy(src, dst, local_sem.at[i])
        copy.start()
        return copy

    fetch_sel = fetch(0, sel_ref, sel_v)
    fetch_cnt = fetch(1, cnt_ref, cnt_v)
    fetch_kvt = fetch(2, kvt_ref, kvt_v)
    first_half = lax.rem(y + 4, NY) // 4
    halves = (first_half, 1 - first_half)

    def fetch_half(i):
        heads = pl.ds(pl.multiple_of(halves[i] * 16, 16), 16)
        return fetch(3 + i, q_ref.at[:, heads, :], q_v.at[i])

    fetch_q = [fetch_half(0)]

    barrier = pltpu.get_barrier_semaphore()
    peers = [partner] + [at_y(k) for k in range(1, NY)] + [at_x(k) for k in range(1, NX)]
    odd = lax.rem(z, 2)
    step = 2 * odd - 1
    twin = z - step
    ahead = (0, 1, -2, 3)
    peers += [at_z((core + 2) * step, c) for c in range(2)]
    peers += [at_z(ahead[i] * step, i % 2) for i in (1, 2, 3)] + [at_z(-step, core)]

    def greet(peer):
        pl.semaphore_signal(barrier, inc=1, device_id=peer, device_id_type=MESH)

    for peer in peers:
        greet(peer)

    @pl.when(core == 1)
    def _():
        for c in range(2):
            greet(at_z(step, c))

    entries = len(peers) + 2 * core

    fetch_sel.wait()
    fetch_cnt.wait()
    r, c = iota((256, 256), 0), iota((256, 256), 1)
    swap = (c == (r & 15) * 16 + (r >> 4)).astype(F32).astype(BF16)

    def by_head(i, g):
        block = q_v[i, g * 16 : (g + 1) * 16].reshape(256, width)
        q_t[pl.ds(halves[i] * 16, 16), g * 16 : (g + 1) * 16, :] = (
            dot(swap, block).astype(BF16).reshape(16, 16, width)
        )

    def between(k):
        if k == 47:
            fetch_kvt.wait()
            fetch_q[0].wait()
            fetch_q.append(fetch_half(1))
        if k >= 48 and k % 4 == 0:
            g = (k - 48) // 4
            by_head(0, g)
            kv_v[:, lane_tiles(LAT)[g]] = kvt_v[g * LANES : (g + 1) * LANES, :].T

    build_bias(sel_v, cnt_v, words, bias, between)

    def dest(u, n):
        return lax.rem(y + (4 - u if n == 0 else u - 4) + NY, NY)

    sequence = ((0, 0), (1, 0), (1, 1), (2, 0), (2, 1), (3, 0), (3, 1), (4, 0))

    def score(i):
        q = q_t[pl.ds(dest(*sequence[i]) * 4, 4)].reshape(256, width)
        s_buf[i % 2] = dot(q, kvt_v[...])

    def compute(i):
        if 0 < i < len(sequence) - 1:
            score(i + 1)
        m = i % 2
        for r in range(0, 256, 16):
            h, qs = r // 64, r % 64
            parts = [s_buf[m, r : r + 16, t] + bias[qs : qs + 16, t] for t in lane_tiles(1024)]
            top = jnp.max(functools.reduce(jnp.maximum, parts), axis=1, keepdims=True)
            weights = [jnp.exp2((part - top) * exp2_scale) for part in parts]
            total = jnp.sum(functools.reduce(jnp.add, weights), axis=1, keepdims=True)
            for t, value in zip(lane_tiles(1024), weights):
                p_buf[m, r : r + 16, t] = value.astype(BF16)
            level = top * softmax_scale + jnp.log(total)
            part[i, h, qs : qs + 16, LAT:] = jnp.broadcast_to(level, (16, LANES))
            inv_buf[m, r : r + 16, :] = jnp.broadcast_to(1.0 / total, (16, LANES))
        o = dot(p_buf[m], kv_v[...])
        for h in range(4):
            inv = inv_buf[m, h * 64 : (h + 1) * 64, :]
            for t in lane_tiles(LAT):
                part[i, h, :, t] = o[h * 64 : (h + 1) * 64, t] * inv

    def pair(u, n):
        i, theirs = sequence.index((u, n)), pl.ds(2 * (1 - core), 2)
        return remote(part.at[i, theirs], pair_in.at[i], pair_send, pair_recv.at[i], partner)

    def pair_start(u, n):
        pair(u, n).start()

    def pair_merge(u, n):
        i = sequence.index((u, n))
        pair(u, n).wait_recv()
        for e in range(2):
            rows = slice(e * 64, (e + 1) * 64)
            mine, theirs = part[i, 2 * core + e, :, LAT:], pair_in[i, e, :, LAT:]
            top = jnp.maximum(mine, theirs)
            a, b = jnp.exp(mine - top), jnp.exp(theirs - top)
            total = a + b
            inv = 1.0 / total
            a, b = a * inv, b * inv
            for t in lane_tiles(LAT):
                own[u, n, rows, t] = part[i, 2 * core + e, :, t] * a + pair_in[i, e, :, t] * b
            own_lse[u, n, rows, :] = top + jnp.log(total)

    sides = (at_y(1), at_y(-1))

    def slot_of(hop, e):
        return 0 if hop == 0 else 2 * hop - 1 + e

    def link(side, i, k):
        out, into = ((stat_out, stat_in), (data_out, data_in))[k]
        return remote(
            out.at[side, i], into.at[side, i],
            ring_send.at[side, k], ring_recv.at[side, i, k], sides[side],
        )

    def incoming(side, i):
        link(side, i, 0).wait_recv()
        return jnp.broadcast_to(stat_in[side, i, 0:1, :], (LANES, LANES)).T[0:64, :]

    def mix(levels):
        top = functools.reduce(jnp.maximum, levels)
        scales = [jnp.exp(level - top) for level in levels]
        total = functools.reduce(jnp.add, scales)
        inv = 1.0 / total
        return [scale * inv for scale in scales], top + jnp.log(total)

    def send(side, hop, e):
        i, n = slot_of(hop, e), 0 if hop == 0 else side
        rows = slice(e * 64, (e + 1) * 64)
        fresh = hop == 0 or (hop == 1 and e != side)
        level = own_lse[hop, n, rows, :]
        if not fresh:
            j = slot_of(hop - 1, e)
            (a, b), level = mix([level, incoming(side, j)])
        stat_out[side, i] = jnp.concatenate([level, level], axis=0).T[0:8, :]
        link(side, i, 0).start()
        if fresh:
            data_out[side, i] = own[hop, n, rows, :].astype(BF16)
        else:
            link(side, j, 1).wait_recv()
            for t in lane_tiles(LAT):
                mixed = own[hop, n, rows, t] * a + data_in[side, j, :, t].astype(F32) * b
                data_out[side, i, :, t] = mixed.astype(BF16)
        link(side, i, 1).start()

    score(0)
    compute(0)
    pl.semaphore_wait(barrier, entries)
    pair_start(0, 0)
    w_twin = remote(w_ref, w_v.at[1], twin_send, twin_recv, {"seq": twin})
    w_twin.start()
    fetch_q[1].wait()
    fetch_up = fetch(5, up_ref, up_v)
    fetch_w = fetch(6, w_ref, w_v.at[0])
    for g in range(Q // 16):
        by_head(1, g)
    score(1)
    pair_merge(0, 0)
    send(0, 0, 0)
    send(1, 0, 1)
    compute(1)
    pair_start(1, 0)
    compute(2)
    pair_start(1, 1)
    pair_merge(1, 0)
    send(0, 1, 1)
    compute(3)
    pair_start(2, 0)
    pair_merge(1, 1)
    send(1, 1, 0)
    send(0, 1, 0)
    send(1, 1, 1)
    compute(4)
    pair_start(2, 1)
    pair_merge(2, 0)
    send(0, 2, 1)
    compute(5)
    pair_start(3, 0)
    pair_merge(2, 1)
    send(1, 2, 0)
    send(0, 2, 0)
    send(1, 2, 1)
    compute(6)
    pair_start(3, 1)
    pair_merge(3, 0)
    send(0, 3, 1)
    compute(7)
    pair_start(4, 0)
    pair_merge(3, 1)
    send(1, 3, 0)
    send(0, 3, 0)
    send(1, 3, 1)

    fetch_w.wait()
    fetch_up.wait()
    pad = jnp.zeros((w_v.shape[1], LANES - BLOCK), BF16)

    def w_copy(m, c):
        return remote(w_all.at[m, c], w_all.at[m, c], w_send.at[m], w_recv.at[m], partner)

    for m in range(2):
        if m == 1:
            w_twin.wait_recv()
        for k, t in enumerate(lane_tiles(8 * LANES)):
            columns = w_v[m, :, k * BLOCK : (k + 1) * BLOCK]
            w_all[m, core, :, t] = jnp.concatenate([columns, pad], axis=1)
        w_copy(m, core).start()

    pair_merge(4, 0)
    for e in (1, 0):
        rows, i = slice(e * 64, (e + 1) * 64), slot_of(3, e)
        (a, b, c), _ = mix([own_lse[4, 0, rows, :], incoming(0, i), incoming(1, i)])
        for side in range(2):
            link(side, i, 1).wait_recv()
        merged = jnp.concatenate(
            [
                own[4, 0, rows, t] * a
                + data_in[0, i, :, t].astype(F32) * b
                + data_in[1, i, :, t].astype(F32) * c
                for t in lane_tiles(LAT)
            ],
            axis=1,
        )
        upper = merged.astype(BF16)
        lower = (merged - upper.astype(F32)).astype(BF16)
        value = dot(upper, up_v[e]) + dot(lower, up_v[e])
        val_v[:, e * VDIM : (e + 1) * VDIM] = value.astype(BF16)


    def at_target(i):
        return at_z(ahead[i] * step, i % 2)

    for i in (3, 2, 1):
        remote(
            val_v, vals.at[i, core], z_send.at[1], z_recv.at[i, core], at_target(i)
        ).start()
    at_pair = remote(val_v, vals.at[0, core], z_send.at[0], z_recv.at[0, core], partner)

    @pl.when(core == 1)
    def _():
        at_pair.start()

    @pl.when(core == 0)
    def _():
        vals[0, 0] = val_v[...]

    def block_of(i):
        return lax.rem(z + step * i + NZ, NZ)

    swap_order = (block_of(core + 2) < block_of(core)).astype(jnp.int32)

    def distance(p):
        return core + 2 * (swap_order if p < 2 else 1 - swap_order)

    def await_half(i, h):
        remote(val_v, vals.at[i, h], z_send.at[0], z_recv.at[i, h], partner).wait_recv()

    for m in range(2):
        w_copy(m, 1 - core).wait_recv()

    def cross(p, k):
        return remote(
            x_out.at[p, k], x_in.at[p, k], x_send.at[p], x_recv.at[p], at_x(k + 1)
        )

    def crossed(p):
        return remote(x_out.at[p], x_in.at[p], x_send.at[p], x_recv.at[p], partner)

    def produce(p):
        i, m = distance(p), p % 2
        if m == 0:

            @pl.when(i != 0)
            def _():
                await_half(i, 0)

            await_half(i, 1)
        terms = dot(vals[i, 0], w_all[m, 0]) + dot(vals[i, 1], w_all[m, 1])
        for k, t in enumerate(lane_tiles(8 * LANES)):
            x_f[p, k] = terms[:, t]
        for k in (0, 2, 1):
            to = lax.rem(x + k + 1, NX)
            for c in range(2):
                x_out[p, k, c] = x_f[p, c * NX + to].astype(BF16)
            cross(p, k).start()

    def spread(p, c):
        column = twin if p % 2 else z
        to = {"ctx": y * 2 + c, "seq": block_of(distance(p))}
        return remote(
            z_out.at[p, c], z_in.at[column], a_send.at[p, c], a_recv.at[column], to
        )

    def consume(p):
        crossed(p).wait_recv()
        for c in range(2):
            total = x_f[p, c * NX + x]
            for k in range(3):
                total = total + x_in[p, k, c].astype(F32)
            z_out[p, c] = total.astype(BF16)
            if c == 0:

                @pl.when(distance(p) == 0)
                def _():
                    z_in[twin if p % 2 else z] = z_out[p, 0]

                @pl.when(distance(p) != 0)
                def _():
                    spread(p, 0).start()

            else:
                spread(p, c).start()

    for p in range(4):
        if p >= 2:
            crossed(p - 2).wait_send()
        produce(p)
    for p in range(4):
        consume(p)

    def last(k):
        to = lax.rem(y + k, NY)
        return remote(z_in.at[to], y_in.at[k], y_send, y_recv, at_y(k))

    for block in range(NZ):

        @pl.when(((block != z) & (block != twin)) | (core == 1))
        def _():
            remote(
                z_out.at[0, 0], z_in.at[block], a_send.at[0, 0], a_recv.at[block], partner
            ).wait_recv()

        k = lax.rem(block - y + NY, NY)

        @pl.when(k != 0)
        def _():
            last(k).start()

    others = y_in.at[1:NY]
    remote(others, others, y_send, y_recv, partner).wait_recv()
    total = z_in[y].astype(F32)
    for k in (1, 7, 2, 6, 3, 5, 4):
        total = total + y_in[k].astype(F32)
    out_ref[...] = total[:, :BLOCK].astype(BF16)

    remote(pair_in, pair_in, pair_send, pair_recv.at[0], partner).wait_send()
    for side in range(2):
        for k, buffer in enumerate((stat_out, data_out)):
            sent = buffer.at[side]
            remote(sent, sent, ring_send.at[side, k], ring_recv.at[side, 0, k], partner).wait_send()
    w_twin.wait_send()
    for m in range(2):
        w_copy(m, core).wait_send()
    three = vals.at[1:4, 0]
    remote(three, three, z_send.at[1], z_recv.at[0, 0], partner).wait_send()

    @pl.when(core == 1)
    def _():
        at_pair.wait_send()

    for p in range(4):
        if p >= 2:
            crossed(p).wait_send()
        spread(p, 1).wait_send()

        @pl.when(distance(p) != 0)
        def _():
            spread(p, 0).wait_send()

    remote(others, others, y_send, y_recv, partner).wait_send()


def shards(queries, latent_cache, selected, counts, value_up, output_proj_weight):
    rows, heads, width = queries.shape
    tokens = latent_cache.shape[0]
    weight = output_proj_weight[0].reshape(2 * VDIM, output_proj_weight.shape[3])
    hbm = pl.BlockSpec(memory_space=pl.ANY)
    vmem, dma = pltpu.VMEM, pltpu.SemaphoreType.DMA
    return pl.pallas_call(
        kernel,
        out_shape=jax.ShapeDtypeStruct((rows, BLOCK), BF16),
        in_specs=[hbm] * 6,
        out_specs=pl.BlockSpec(memory_space=pltpu.VMEM),
        scratch_shapes=[
            vmem(selected.shape, jnp.int32),
            vmem((1, rows), jnp.int32),
            vmem((2, rows, 16, width), BF16),
            vmem((width, tokens), BF16),
            vmem((2, LAT, VDIM), BF16),
            vmem((2,) + weight.shape, BF16),
            dma((7,)),
            vmem((64, LANES), F32),
            vmem((rows, tokens), F32),
            vmem((tokens, LAT), BF16),
            vmem((heads, rows, width), BF16),
            vmem((2, 256, tokens), F32),
            vmem((2, 256, tokens), BF16),
            vmem((2, 256, LANES), F32),
            vmem((8, 4, rows, LAT + LANES), F32),
            vmem((8, 2, rows, LAT + LANES), F32),
            dma,
            dma((8,)),
            vmem((5, 2, 2 * rows, LAT), F32),
            vmem((5, 2, 2 * rows, LANES), F32),
            vmem((2, 7, rows, LAT), BF16),
            vmem((2, 7, rows, LAT), BF16),
            vmem((2, 7, 8, LANES), F32),
            vmem((2, 7, 8, LANES), F32),
            dma((2, 2)),
            dma((2, 7, 2)),
            vmem((rows, 2 * VDIM), BF16),
            vmem((4, 2, rows, 2 * VDIM), BF16),
            vmem((2, 2, 2 * VDIM, 8 * LANES), BF16),
            dma((2,)),
            dma((2,)),
            dma,
            dma,
            dma((2,)),
            dma((4, 2)),
            vmem((4, 8, rows, LANES), F32),
            vmem((4, 3, 2, rows, LANES), BF16),
            vmem((4, 3, 2, rows, LANES), BF16),
            dma((4,)),
            dma((4,)),
            vmem((4, 2, rows, LANES), BF16),
            vmem((NZ, rows, LANES), BF16),
            dma((4, 2)),
            dma((NZ,)),
            vmem((NY, rows, LANES), BF16),
            dma,
            dma,
        ],
        compiler_params=pltpu.CompilerParams(
            collective_id=0, has_side_effects=True, vmem_limit_bytes=60 * 1024 * 1024
        ),
    )(selected, counts.T, queries, latent_cache.T, value_up[0], weight)


def solution(mesh):
    in_specs = (
        P("seq", "head", None),
        P("ctx", None),
        P("seq", "ctx", None),
        P("seq", "ctx"),
        P("head", "ctx", None, None),
        P("head", "ctx", None, "seq"),
    )
    out_specs = P("seq", ("ctx", "head"))
    return jax.shard_map(shards, mesh=mesh, in_specs=in_specs, out_specs=out_specs, check_vma=False)
```

```python
import functools
import math

import jax
import jax.numpy as jnp
from jax import lax
from jax.experimental import pallas as pl
from jax.experimental.pallas import tpu as pltpu
from jax.sharding import PartitionSpec as P

LAT = 512
VDIM = 128
LANES = 128
FAR = 1e30
MESH = pl.DeviceIdType.MESH
NY = 8
NZ = 8
NX = 4
Q = 64
BLOCK = 112
F32 = jnp.float32
BF16 = jnp.bfloat16

softmax_scale = (0.1 * math.log(40.0) + 1.0) ** 2 / math.sqrt(192.0)
exp2_scale = softmax_scale / math.log(2.0)


def iota(shape, axis):
    return lax.broadcasted_iota(jnp.int32, shape, axis)


def dot(a, b):
    return jnp.dot(a, b, preferred_element_type=F32)


def remote(src, dst, s, r, peer):
    return pltpu.make_async_remote_copy(
        src_ref=src, dst_ref=dst, send_sem=s, recv_sem=r, device_id=peer, device_id_type=MESH
    )


def lane_tiles(width):
    return [slice(t * LANES, (t + 1) * LANES) for t in range(width // LANES)]


def build_bias(sel_v, cnt_v, words, bias, between):
    tokens = bias.shape[1]
    lane = iota((1, LANES), 1)
    s = sel_v[...].reshape(Q, 384).astype(F32)
    first = jnp.concatenate([s[:, 0:128], s[:, 128:256]], axis=0).T
    last = jnp.concatenate([s[:, 256:384], s[:, 256:384]], axis=0).T
    last = jnp.where(lane < 64, last[0:64], last[64:128])
    sel_t = jnp.concatenate([first, last], axis=0).astype(jnp.int32)
    row = iota((192, LANES), 0)
    late = (iota((192, LANES), 1) >= 64).astype(jnp.int32)
    slot = jnp.where(row < 128, row + 128 * late, row + 128 + 64 * late)
    cnt = cnt_v[...]
    cnt = jnp.concatenate([cnt, cnt], axis=1)
    high = sel_t >> 4
    value = jnp.where(slot < cnt, (1 << (sel_t & 15)).astype(F32), 0.0)
    for k in range(64):
        words[k : k + 1, :] = jnp.sum(jnp.where(high == k, value, 0.0), axis=0, keepdims=True)
        between(k)
    w = words[...]
    w = (w + pltpu.roll(w, 64, 1)).astype(jnp.int32)
    bytes_t = jnp.concatenate([(w & 255).astype(F32), (w >> 8).astype(F32)], axis=0).T
    token = iota((128, tokens), 1)
    place = ((token >> 3) & 1) * 64 + (token >> 4)
    expand = (place == iota((128, tokens), 0)).astype(F32).astype(BF16)
    found = dot(bytes_t[0:Q].astype(BF16), expand).astype(jnp.int32)
    bit = (found >> (iota((Q, tokens), 1) & 7)) & 1
    bias[...] = jnp.where(bit == 1, 0.0, -FAR)


def kernel(
    sel_ref, cnt_ref, q_ref, kvt_ref, up_ref, w_ref, out_ref,
    sel_v, cnt_v, q_v, kvt_v, up_v, w_v, local_sem,
    words, bias, kv_v, q_t, s_buf, p_buf, inv_buf,
    part, pair_in, pair_send, pair_recv, own, own_lse,
    data_out, data_in, stat_out, stat_in, ring_send, ring_recv,
    val_v, vals, w_all, w_send, w_recv, twin_send, twin_recv, z_send, z_recv,
    x_f, x_out, x_in, x_send, x_recv, z_out, z_in, a_send, a_recv, y_in, y_send, y_recv,
):
    width = kvt_ref.shape[0]
    ctx, x, z = lax.axis_index("ctx"), lax.axis_index("head"), lax.axis_index("seq")
    y, core = ctx // 2, lax.rem(ctx, 2)
    partner = {"ctx": y * 2 + 1 - core}

    def at_y(k):
        return {"ctx": lax.rem(y + k + NY, NY) * 2 + core}

    def at_z(k, c):
        return {"ctx": y * 2 + c, "seq": lax.rem(z + k + NZ, NZ)}

    def at_x(k):
        return {"head": lax.rem(x + k, NX)}

    def fetch(i, src, dst):
        copy = pltpu.make_async_copy(src, dst, local_sem.at[i])
        copy.start()
        return copy

    fetch_sel = fetch(0, sel_ref, sel_v)
    fetch_cnt = fetch(1, cnt_ref, cnt_v)
    fetch_kvt = fetch(2, kvt_ref, kvt_v)
    first_half = lax.rem(y + 4, NY) // 4
    halves = (first_half, 1 - first_half)

    def fetch_half(i):
        heads = pl.ds(pl.multiple_of(halves[i] * 16, 16), 16)
        return fetch(3 + i, q_ref.at[:, heads, :], q_v.at[i])

    fetch_q = [fetch_half(0)]

    barrier = pltpu.get_barrier_semaphore()
    peers = [partner] + [at_y(k) for k in range(1, NY)] + [at_x(k) for k in range(1, NX)]
    odd = lax.rem(z, 2)
    step = 2 * odd - 1
    twin = z - step
    ahead = (0, 1, -2, 3)
    peers += [at_z((core + 2) * step, c) for c in range(2)]
    peers += [at_z(ahead[i] * step, i % 2) for i in (1, 2, 3)] + [at_z(-step, core)]

    def greet(peer):
        pl.semaphore_signal(barrier, inc=1, device_id=peer, device_id_type=MESH)

    for peer in peers:
        greet(peer)

    @pl.when(core == 1)
    def _():
        for c in range(2):
            greet(at_z(step, c))

    entries = len(peers) + 2 * core

    fetch_sel.wait()
    fetch_cnt.wait()
    r, c = iota((256, 256), 0), iota((256, 256), 1)
    swap = (c == (r & 15) * 16 + (r >> 4)).astype(F32).astype(BF16)

    def by_head(i, g):
        block = q_v[i, g * 16 : (g + 1) * 16].reshape(256, width)
        q_t[pl.ds(halves[i] * 16, 16), g * 16 : (g + 1) * 16, :] = (
            dot(swap, block).astype(BF16).reshape(16, 16, width)
        )

    def between(k):
        if k == 47:
            fetch_kvt.wait()
            fetch_q[0].wait()
            fetch_q.append(fetch_half(1))
        if k >= 48 and k % 4 == 0:
            g = (k - 48) // 4
            by_head(0, g)
            kv_v[:, lane_tiles(LAT)[g]] = kvt_v[g * LANES : (g + 1) * LANES, :].T

    build_bias(sel_v, cnt_v, words, bias, between)

    def dest(u, n):
        return lax.rem(y + (4 - u if n == 0 else u - 4) + NY, NY)

    sequence = ((0, 0), (1, 0), (1, 1), (2, 0), (2, 1), (3, 0), (3, 1), (4, 0))

    def score(i):
        q = q_t[pl.ds(dest(*sequence[i]) * 4, 4)].reshape(256, width)
        s_buf[i % 2] = dot(q, kvt_v[...])

    def compute(i):
        if 0 < i < len(sequence) - 1:
            score(i + 1)
        m = i % 2
        for r in range(0, 256, 16):
            h, qs = r // 64, r % 64
            parts = [s_buf[m, r : r + 16, t] + bias[qs : qs + 16, t] for t in lane_tiles(1024)]
            top = jnp.max(functools.reduce(jnp.maximum, parts), axis=1, keepdims=True)
            weights = [jnp.exp2((part - top) * exp2_scale) for part in parts]
            total = jnp.sum(functools.reduce(jnp.add, weights), axis=1, keepdims=True)
            for t, value in zip(lane_tiles(1024), weights):
                p_buf[m, r : r + 16, t] = value.astype(BF16)
            level = top * softmax_scale + jnp.log(total)
            part[i, h, qs : qs + 16, LAT:] = jnp.broadcast_to(level, (16, LANES))
            inv_buf[m, r : r + 16, :] = jnp.broadcast_to(1.0 / total, (16, LANES))
        o = dot(p_buf[m], kv_v[...])
        for h in range(4):
            inv = inv_buf[m, h * 64 : (h + 1) * 64, :]
            for t in lane_tiles(LAT):
                part[i, h, :, t] = o[h * 64 : (h + 1) * 64, t] * inv

    def pair(u, n):
        i, theirs = sequence.index((u, n)), pl.ds(2 * (1 - core), 2)
        return remote(part.at[i, theirs], pair_in.at[i], pair_send, pair_recv.at[i], partner)

    def pair_start(u, n):
        pair(u, n).start()

    def pair_merge(u, n):
        i = sequence.index((u, n))
        pair(u, n).wait_recv()
        for e in range(2):
            rows = slice(e * 64, (e + 1) * 64)
            mine, theirs = part[i, 2 * core + e, :, LAT:], pair_in[i, e, :, LAT:]
            top = jnp.maximum(mine, theirs)
            a, b = jnp.exp(mine - top), jnp.exp(theirs - top)
            total = a + b
            inv = 1.0 / total
            a, b = a * inv, b * inv
            for t in lane_tiles(LAT):
                own[u, n, rows, t] = part[i, 2 * core + e, :, t] * a + pair_in[i, e, :, t] * b
            own_lse[u, n, rows, :] = top + jnp.log(total)

    sides = (at_y(1), at_y(-1))

    def slot_of(hop, e):
        return 0 if hop == 0 else 2 * hop - 1 + e

    def link(side, i, k):
        out, into = ((stat_out, stat_in), (data_out, data_in))[k]
        return remote(
            out.at[side, i], into.at[side, i],
            ring_send.at[side, k], ring_recv.at[side, i, k], sides[side],
        )

    def incoming(side, i):
        link(side, i, 0).wait_recv()
        return jnp.broadcast_to(stat_in[side, i, 0:1, :], (LANES, LANES)).T[0:64, :]

    def mix(levels):
        top = functools.reduce(jnp.maximum, levels)
        scales = [jnp.exp(level - top) for level in levels]
        total = functools.reduce(jnp.add, scales)
        inv = 1.0 / total
        return [scale * inv for scale in scales], top + jnp.log(total)

    def send(side, hop, e):
        i, n = slot_of(hop, e), 0 if hop == 0 else side
        rows = slice(e * 64, (e + 1) * 64)
        fresh = hop == 0 or (hop == 1 and e != side)
        level = own_lse[hop, n, rows, :]
        if not fresh:
            j = slot_of(hop - 1, e)
            (a, b), level = mix([level, incoming(side, j)])
        else:
            data_out[side, i] = own[hop, n, rows, :].astype(BF16)
            link(side, i, 1).start()
        stat_out[side, i] = jnp.concatenate([level, level], axis=0).T[0:8, :]
        link(side, i, 0).start()
        if not fresh:
            link(side, j, 1).wait_recv()
            for t in lane_tiles(LAT):
                mixed = own[hop, n, rows, t] * a + data_in[side, j, :, t].astype(F32) * b
                data_out[side, i, :, t] = mixed.astype(BF16)
            link(side, i, 1).start()

    score(0)
    compute(0)
    pl.semaphore_wait(barrier, entries)
    pair_start(0, 0)
    w_twin = remote(w_ref, w_v.at[1], twin_send, twin_recv, {"seq": twin})
    w_twin.start()
    fetch_q[1].wait()
    fetch_up = fetch(5, up_ref, up_v)
    fetch_w = fetch(6, w_ref, w_v.at[0])
    for g in range(Q // 16):
        by_head(1, g)
    score(1)
    pair_merge(0, 0)
    send(0, 0, 0)
    send(1, 0, 1)
    compute(1)
    pair_start(1, 0)
    compute(2)
    pair_start(1, 1)
    pair_merge(1, 0)
    send(0, 1, 1)
    compute(3)
    pair_start(2, 0)
    pair_merge(1, 1)
    send(1, 1, 0)
    send(0, 1, 0)
    send(1, 1, 1)
    compute(4)
    pair_start(2, 1)
    pair_merge(2, 0)
    send(0, 2, 1)
    compute(5)
    pair_start(3, 0)
    pair_merge(2, 1)
    send(1, 2, 0)
    send(0, 2, 0)
    send(1, 2, 1)
    compute(6)
    pair_start(3, 1)
    pair_merge(3, 0)
    send(0, 3, 1)
    compute(7)
    pair_start(4, 0)
    pair_merge(3, 1)
    send(1, 3, 0)
    send(0, 3, 0)
    send(1, 3, 1)

    fetch_w.wait()
    fetch_up.wait()
    pad = jnp.zeros((w_v.shape[1], LANES - BLOCK), BF16)

    def w_copy(m, c):
        return remote(w_all.at[m, c], w_all.at[m, c], w_send, w_recv, partner)

    for m in range(2):
        if m == 1:
            w_twin.wait_recv()
        for k, t in enumerate(lane_tiles(8 * LANES)):
            columns = w_v[m, :, k * BLOCK : (k + 1) * BLOCK]
            w_all[m, core, :, t] = jnp.concatenate([columns, pad], axis=1)
        w_copy(m, core).start()

    pair_merge(4, 0)
    for e in (1, 0):
        rows, i = slice(e * 64, (e + 1) * 64), slot_of(3, e)
        (a, b, c), _ = mix([own_lse[4, 0, rows, :], incoming(0, i), incoming(1, i)])
        for side in range(2):
            link(side, i, 1).wait_recv()
        merged = jnp.concatenate(
            [
                own[4, 0, rows, t] * a
                + data_in[0, i, :, t].astype(F32) * b
                + data_in[1, i, :, t].astype(F32) * c
                for t in lane_tiles(LAT)
            ],
            axis=1,
        )
        upper = merged.astype(BF16)
        lower = (merged - upper.astype(F32)).astype(BF16)
        value = dot(upper, up_v[e]) + dot(lower, up_v[e])
        val_v[:, e * VDIM : (e + 1) * VDIM] = value.astype(BF16)


    def at_target(i):
        return at_z(ahead[i] * step, i % 2)

    for i in (3, 2, 1):
        remote(
            val_v, vals.at[i, core], z_send.at[1], z_recv.at[i], at_target(i)
        ).start()
    at_pair = remote(val_v, vals.at[0, core], z_send.at[0], z_recv.at[0], partner)

    @pl.when(core == 1)
    def _():
        at_pair.start()

    @pl.when(core == 0)
    def _():
        vals[0, 0] = val_v[...]

    def block_of(i):
        return lax.rem(z + step * i + NZ, NZ)

    swap_order = (block_of(core + 2) < block_of(core)).astype(jnp.int32)

    def distance(p):
        return core + 2 * (swap_order if p < 2 else 1 - swap_order)

    def await_values(i, into):
        remote(into, into, z_send.at[0], z_recv.at[i], partner).wait_recv()

    both = w_all.at[0]
    remote(both, both, w_send, w_recv, partner).wait_recv()

    def cross(p, k):
        return remote(
            x_out.at[p, k], x_in.at[p, k], x_send.at[p], x_recv.at[p], at_x(k + 1)
        )

    def crossed(p):
        return remote(x_out.at[p], x_in.at[p], x_send.at[p], x_recv.at[p], partner)

    def produce(p):
        i, m = distance(p), p % 2
        if m == 0:

            @pl.when(i != 0)
            def _():
                await_values(i, vals.at[i])

            @pl.when(i == 0)
            def _():
                await_values(0, vals.at[0, 1])

        terms = dot(vals[i, 0], w_all[m, 0]) + dot(vals[i, 1], w_all[m, 1])
        for k, t in enumerate(lane_tiles(8 * LANES)):
            x_f[p, k] = terms[:, t]
        for k in (0, 2, 1):
            to = lax.rem(x + k + 1, NX)
            for c in range(2):
                x_out[p, k, c] = x_f[p, c * NX + to].astype(BF16)
            cross(p, k).start()

    def spread(p, c):
        column = twin if p % 2 else z
        to = {"ctx": y * 2 + c, "seq": block_of(distance(p))}
        return remote(
            z_out.at[p, c], z_in.at[column], a_send.at[4 if c else p], a_recv.at[column], to
        )

    def consume(p):
        crossed(p).wait_recv()
        for c in range(2):
            total = x_f[p, c * NX + x]
            for k in range(3):
                total = total + x_in[p, k, c].astype(F32)
            z_out[p, c] = total.astype(BF16)
            if c == 0:

                @pl.when(distance(p) == 0)
                def _():
                    z_in[twin if p % 2 else z] = z_out[p, 0]

                @pl.when(distance(p) != 0)
                def _():
                    spread(p, 0).start()

            else:
                spread(p, c).start()

    for p in range(4):
        if p >= 2:
            crossed(p - 2).wait_send()
        produce(p)
    for p in range(4):
        consume(p)

    def last(k):
        to = lax.rem(y + k, NY)
        return remote(z_in.at[to], y_in.at[k], y_send, y_recv, at_y(k))

    for block in range(NZ):

        @pl.when(((block != z) & (block != twin)) | (core == 1))
        def _():
            remote(
                z_out.at[0, 0], z_in.at[block], a_send.at[0], a_recv.at[block], partner
            ).wait_recv()

        k = lax.rem(block - y + NY, NY)

        @pl.when(k != 0)
        def _():
            last(k).start()

    others = y_in.at[1:NY]
    remote(others, others, y_send, y_recv, partner).wait_recv()
    total = z_in[y].astype(F32)
    for k in (1, 7, 2, 6, 3, 5, 4):
        total = total + y_in[k].astype(F32)
    out_ref[...] = total[:, :BLOCK].astype(BF16)

    remote(pair_in, pair_in, pair_send, pair_recv.at[0], partner).wait_send()
    for side in range(2):
        for k, buffer in enumerate((stat_out, data_out)):
            sent = buffer.at[side]
            remote(sent, sent, ring_send.at[side, k], ring_recv.at[side, 0, k], partner).wait_send()
    w_twin.wait_send()
    remote(both, both, w_send, w_recv, partner).wait_send()
    three = vals.at[1:4, 0]
    remote(three, three, z_send.at[1], z_recv.at[0], partner).wait_send()

    @pl.when(core == 1)
    def _():
        at_pair.wait_send()

    for p in range(4):
        if p >= 2:
            crossed(p).wait_send()
        @pl.when(distance(p) != 0)
        def _():
            spread(p, 0).wait_send()

    remote(others, others, y_send, y_recv, partner).wait_send()
    second = z_out.at[:, 1]
    remote(second, second, a_send.at[4], a_recv.at[0], partner).wait_send()


def shards(queries, latent_cache, selected, counts, value_up, output_proj_weight):
    rows, heads, width = queries.shape
    tokens = latent_cache.shape[0]
    weight = output_proj_weight[0].reshape(2 * VDIM, output_proj_weight.shape[3])
    hbm = pl.BlockSpec(memory_space=pl.ANY)
    vmem, dma = pltpu.VMEM, pltpu.SemaphoreType.DMA
    return pl.pallas_call(
        kernel,
        out_shape=jax.ShapeDtypeStruct((rows, BLOCK), BF16),
        in_specs=[hbm] * 6,
        out_specs=pl.BlockSpec(memory_space=pltpu.VMEM),
        scratch_shapes=[
            vmem(selected.shape, jnp.int32),
            vmem((1, rows), jnp.int32),
            vmem((2, rows, 16, width), BF16),
            vmem((width, tokens), BF16),
            vmem((2, LAT, VDIM), BF16),
            vmem((2,) + weight.shape, BF16),
            dma((7,)),
            vmem((64, LANES), F32),
            vmem((rows, tokens), F32),
            vmem((tokens, LAT), BF16),
            vmem((heads, rows, width), BF16),
            vmem((2, 256, tokens), F32),
            vmem((2, 256, tokens), BF16),
            vmem((2, 256, LANES), F32),
            vmem((8, 4, rows, LAT + LANES), F32),
            vmem((8, 2, rows, LAT + LANES), F32),
            dma,
            dma((8,)),
            vmem((5, 2, 2 * rows, LAT), F32),
            vmem((5, 2, 2 * rows, LANES), F32),
            vmem((2, 7, rows, LAT), BF16),
            vmem((2, 7, rows, LAT), BF16),
            vmem((2, 7, 8, LANES), F32),
            vmem((2, 7, 8, LANES), F32),
            dma((2, 2)),
            dma((2, 7, 2)),
            vmem((rows, 2 * VDIM), BF16),
            vmem((4, 2, rows, 2 * VDIM), BF16),
            vmem((2, 2, 2 * VDIM, 8 * LANES), BF16),
            dma,
            dma,
            dma,
            dma,
            dma((2,)),
            dma((4,)),
            vmem((4, 8, rows, LANES), F32),
            vmem((4, 3, 2, rows, LANES), BF16),
            vmem((4, 3, 2, rows, LANES), BF16),
            dma((4,)),
            dma((4,)),
            vmem((4, 2, rows, LANES), BF16),
            vmem((NZ, rows, LANES), BF16),
            dma((5,)),
            dma((NZ,)),
            vmem((NY, rows, LANES), BF16),
            dma,
            dma,
        ],
        compiler_params=pltpu.CompilerParams(
            collective_id=0, has_side_effects=True, vmem_limit_bytes=60 * 1024 * 1024
        ),
    )(selected, counts.T, queries, latent_cache.T, value_up[0], weight)


def solution(mesh):
    in_specs = (
        P("seq", "head", None),
        P("ctx", None),
        P("seq", "ctx", None),
        P("seq", "ctx"),
        P("head", "ctx", None, None),
        P("head", "ctx", None, "seq"),
    )
    out_specs = P("seq", ("ctx", "head"))
    return jax.shard_map(shards, mesh=mesh, in_specs=in_specs, out_specs=out_specs, check_vma=False)
```

```python
import functools
import math

import jax
import jax.numpy as jnp
from jax import lax
from jax.experimental import pallas as pl
from jax.experimental.pallas import tpu as pltpu
from jax.sharding import PartitionSpec as P

LAT = 512
VDIM = 128
LANES = 128
FAR = 1e30
MESH = pl.DeviceIdType.MESH
NY = 8
NZ = 8
NX = 4
Q = 64
BLOCK = 112
F32 = jnp.float32
BF16 = jnp.bfloat16

softmax_scale = (0.1 * math.log(40.0) + 1.0) ** 2 / math.sqrt(192.0)
exp2_scale = softmax_scale / math.log(2.0)


def iota(shape, axis):
    return lax.broadcasted_iota(jnp.int32, shape, axis)


def dot(a, b):
    return jnp.dot(a, b, preferred_element_type=F32)


def remote(src, dst, s, r, peer):
    return pltpu.make_async_remote_copy(
        src_ref=src, dst_ref=dst, send_sem=s, recv_sem=r, device_id=peer, device_id_type=MESH
    )


def lane_tiles(width):
    return [slice(t * LANES, (t + 1) * LANES) for t in range(width // LANES)]


def build_bias(sel_v, cnt_v, words, bias, between):
    tokens = bias.shape[1]
    lane = iota((1, LANES), 1)
    s = sel_v[...].reshape(Q, 384).astype(F32)
    first = jnp.concatenate([s[:, 0:128], s[:, 128:256]], axis=0).T
    last = jnp.concatenate([s[:, 256:384], s[:, 256:384]], axis=0).T
    last = jnp.where(lane < 64, last[0:64], last[64:128])
    sel_t = jnp.concatenate([first, last], axis=0).astype(jnp.int32)
    row = iota((192, LANES), 0)
    late = (iota((192, LANES), 1) >= 64).astype(jnp.int32)
    slot = jnp.where(row < 128, row + 128 * late, row + 128 + 64 * late)
    cnt = cnt_v[...]
    cnt = jnp.concatenate([cnt, cnt], axis=1)
    high = sel_t >> 4
    value = jnp.where(slot < cnt, (1 << (sel_t & 15)).astype(F32), 0.0)
    for k in range(64):
        words[k : k + 1, :] = jnp.sum(jnp.where(high == k, value, 0.0), axis=0, keepdims=True)
        between(k)
    w = words[...]
    w = (w + pltpu.roll(w, 64, 1)).astype(jnp.int32)
    bytes_t = jnp.concatenate([(w & 255).astype(F32), (w >> 8).astype(F32)], axis=0).T
    token = iota((128, tokens), 1)
    place = ((token >> 3) & 1) * 64 + (token >> 4)
    expand = (place == iota((128, tokens), 0)).astype(F32).astype(BF16)
    found = dot(bytes_t[0:Q].astype(BF16), expand).astype(jnp.int32)
    bit = (found >> (iota((Q, tokens), 1) & 7)) & 1
    bias[...] = jnp.where(bit == 1, 0.0, -FAR)


def kernel(
    sel_ref, cnt_ref, q_ref, kvt_ref, up_ref, w_ref, out_ref,
    sel_v, cnt_v, q_v, kvt_v, up_v, w_v, local_sem,
    words, bias, kv_v, q_t, s_buf, p_buf, inv_buf,
    part, pair_in, pair_send, pair_recv, own, own_lse,
    data_out, data_in, stat_out, stat_in, ring_send, ring_recv,
    val_v, vals, w_all, w_send, w_recv, twin_send, twin_recv, z_send, z_recv,
    x_f, x_out, x_in, x_send, x_recv, z_out, z_in, a_send, a_recv, y_in, y_send, y_recv,
):
    width = kvt_ref.shape[0]
    ctx, x, z = lax.axis_index("ctx"), lax.axis_index("head"), lax.axis_index("seq")
    y, core = ctx // 2, lax.rem(ctx, 2)
    partner = {"ctx": y * 2 + 1 - core}

    def at_y(k):
        return {"ctx": lax.rem(y + k + NY, NY) * 2 + core}

    def at_z(k, c):
        return {"ctx": y * 2 + c, "seq": lax.rem(z + k + NZ, NZ)}

    def at_x(k):
        return {"head": lax.rem(x + k, NX)}

    def fetch(i, src, dst):
        copy = pltpu.make_async_copy(src, dst, local_sem.at[i])
        copy.start()
        return copy

    fetch_sel = fetch(0, sel_ref, sel_v)
    fetch_cnt = fetch(1, cnt_ref, cnt_v)
    fetch_kvt = fetch(2, kvt_ref, kvt_v)
    first_half = lax.rem(y + 4, NY) // 4
    halves = (first_half, 1 - first_half)

    def fetch_half(i):
        heads = pl.ds(pl.multiple_of(halves[i] * 16, 16), 16)
        return fetch(3 + i, q_ref.at[:, heads, :], q_v.at[i])

    fetch_q = [fetch_half(0)]

    barrier = pltpu.get_barrier_semaphore()
    peers = [partner] + [at_y(k) for k in range(1, NY)] + [at_x(k) for k in range(1, NX)]
    odd = lax.rem(z, 2)
    step = 2 * odd - 1
    twin = z - step
    ahead = (0, 1, -2, 3)
    peers += [at_z((core + 2) * step, c) for c in range(2)]
    peers += [at_z(ahead[i] * step, i % 2) for i in (1, 2, 3)] + [at_z(-step, core)]

    def greet(peer):
        pl.semaphore_signal(barrier, inc=1, device_id=peer, device_id_type=MESH)

    for peer in peers:
        greet(peer)

    @pl.when(core == 1)
    def _():
        for c in range(2):
            greet(at_z(step, c))

    entries = len(peers) + 2 * core

    fetch_sel.wait()
    fetch_cnt.wait()
    r, c = iota((256, 256), 0), iota((256, 256), 1)
    swap = (c == (r & 15) * 16 + (r >> 4)).astype(F32).astype(BF16)

    def by_head(i, g):
        block = q_v[i, g * 16 : (g + 1) * 16].reshape(256, width)
        q_t[pl.ds(halves[i] * 16, 16), g * 16 : (g + 1) * 16, :] = (
            dot(swap, block).astype(BF16).reshape(16, 16, width)
        )

    def between(k):
        if k == 47:
            fetch_kvt.wait()
            fetch_q[0].wait()
            fetch_q.append(fetch_half(1))
        if k >= 48 and k % 4 == 0:
            g = (k - 48) // 4
            by_head(0, g)
            kv_v[:, lane_tiles(LAT)[g]] = kvt_v[g * LANES : (g + 1) * LANES, :].T

    build_bias(sel_v, cnt_v, words, bias, between)

    def dest(u, n):
        return lax.rem(y + (4 - u if n == 0 else u - 4) + NY, NY)

    sequence = ((0, 0), (1, 0), (1, 1), (2, 0), (2, 1), (3, 0), (3, 1), (4, 0))

    def score(i):
        q = q_t[pl.ds(dest(*sequence[i]) * 4, 4)].reshape(256, width)
        s_buf[i % 2] = dot(q, kvt_v[...])

    def compute(i):
        if 0 < i < len(sequence) - 1:
            score(i + 1)
        m = i % 2
        for r in range(0, 256, 16):
            h, qs = r // 64, r % 64
            parts = [s_buf[m, r : r + 16, t] + bias[qs : qs + 16, t] for t in lane_tiles(1024)]
            top = jnp.max(functools.reduce(jnp.maximum, parts), axis=1, keepdims=True)
            weights = [jnp.exp2((part - top) * exp2_scale) for part in parts]
            total = jnp.sum(functools.reduce(jnp.add, weights), axis=1, keepdims=True)
            for t, value in zip(lane_tiles(1024), weights):
                p_buf[m, r : r + 16, t] = value.astype(BF16)
            level = top * softmax_scale + jnp.log(total)
            part[i, h, qs : qs + 16, LAT:] = jnp.broadcast_to(level, (16, LANES))
            inv_buf[m, r : r + 16, :] = jnp.broadcast_to(1.0 / total, (16, LANES))
        o = dot(p_buf[m], kv_v[...])
        for h in range(4):
            inv = inv_buf[m, h * 64 : (h + 1) * 64, :]
            for t in lane_tiles(LAT):
                part[i, h, :, t] = o[h * 64 : (h + 1) * 64, t] * inv

    def pair(u, n):
        i, theirs = sequence.index((u, n)), pl.ds(2 * (1 - core), 2)
        return remote(part.at[i, theirs], pair_in.at[i], pair_send, pair_recv.at[i], partner)

    def pair_start(u, n):
        pair(u, n).start()

    def pair_merge(u, n):
        i = sequence.index((u, n))
        pair(u, n).wait_recv()
        for e in range(2):
            rows = slice(e * 64, (e + 1) * 64)
            mine, theirs = part[i, 2 * core + e, :, LAT:], pair_in[i, e, :, LAT:]
            top = jnp.maximum(mine, theirs)
            a, b = jnp.exp(mine - top), jnp.exp(theirs - top)
            total = a + b
            inv = 1.0 / total
            a, b = a * inv, b * inv
            for t in lane_tiles(LAT):
                own[u, n, rows, t] = part[i, 2 * core + e, :, t] * a + pair_in[i, e, :, t] * b
            own_lse[u, n, rows, :] = top + jnp.log(total)

    sides = (at_y(1), at_y(-1))

    def slot_of(hop, e):
        return 0 if hop == 0 else 2 * hop - 1 + e

    def link(side, i, k):
        out, into = ((stat_out, stat_in), (data_out, data_in))[k]
        return remote(
            out.at[side, i], into.at[side, i],
            ring_send.at[side, k], ring_recv.at[side, i, k], sides[side],
        )

    def incoming(side, i):
        link(side, i, 0).wait_recv()
        return jnp.broadcast_to(stat_in[side, i, 0:1, :], (LANES, LANES)).T[0:64, :]

    def mix(levels):
        top = functools.reduce(jnp.maximum, levels)
        scales = [jnp.exp(level - top) for level in levels]
        total = functools.reduce(jnp.add, scales)
        inv = 1.0 / total
        return [scale * inv for scale in scales], top + jnp.log(total)

    def send(side, hop, e):
        i, n = slot_of(hop, e), 0 if hop == 0 else side
        rows = slice(e * 64, (e + 1) * 64)
        fresh = hop == 0 or (hop == 1 and e != side)
        level = own_lse[hop, n, rows, :]
        if not fresh:
            j = slot_of(hop - 1, e)
            (a, b), level = mix([level, incoming(side, j)])
        stat_out[side, i] = jnp.concatenate([level, level], axis=0).T[0:8, :]
        link(side, i, 0).start()
        if fresh:
            data_out[side, i] = own[hop, n, rows, :].astype(BF16)
        else:
            link(side, j, 1).wait_recv()
            for t in lane_tiles(LAT):
                mixed = own[hop, n, rows, t] * a + data_in[side, j, :, t].astype(F32) * b
                data_out[side, i, :, t] = mixed.astype(BF16)
        link(side, i, 1).start()

    score(0)
    compute(0)
    pl.semaphore_wait(barrier, entries)
    pair_start(0, 0)
    w_twin = remote(w_ref, w_v.at[1], twin_send, twin_recv, {"seq": twin})
    w_twin.start()
    fetch_q[1].wait()
    fetch_up = fetch(5, up_ref, up_v)
    fetch_w = fetch(6, w_ref, w_v.at[0])
    for g in range(Q // 16):
        by_head(1, g)
    score(1)
    pair_merge(0, 0)
    send(0, 0, 0)
    send(1, 0, 1)
    compute(1)
    pair_start(1, 0)
    compute(2)
    pair_start(1, 1)
    pair_merge(1, 0)
    send(0, 1, 1)
    compute(3)
    pair_start(2, 0)
    pair_merge(1, 1)
    send(1, 1, 0)
    send(0, 1, 0)
    send(1, 1, 1)
    compute(4)
    pair_start(2, 1)
    pair_merge(2, 0)
    send(0, 2, 1)
    compute(5)
    pair_start(3, 0)
    pair_merge(2, 1)
    send(1, 2, 0)
    send(0, 2, 0)
    send(1, 2, 1)
    compute(6)
    pair_start(3, 1)
    pair_merge(3, 0)
    send(0, 3, 1)
    compute(7)
    pair_start(4, 0)
    pair_merge(3, 1)
    send(1, 3, 0)
    send(0, 3, 0)
    send(1, 3, 1)

    fetch_w.wait()
    fetch_up.wait()
    pad = jnp.zeros((w_v.shape[1], LANES - BLOCK), BF16)

    def w_copy(m, c):
        return remote(w_all.at[m, c], w_all.at[m, c], w_send.at[m], w_recv.at[m], partner)

    for m in range(2):
        if m == 1:
            w_twin.wait_recv()
        for k, t in enumerate(lane_tiles(8 * LANES)):
            columns = w_v[m, :, k * BLOCK : (k + 1) * BLOCK]
            w_all[m, core, :, t] = jnp.concatenate([columns, pad], axis=1)
        w_copy(m, core).start()

    pair_merge(4, 0)
    for e in (1, 0):
        rows, i = slice(e * 64, (e + 1) * 64), slot_of(3, e)
        (a, b, c), _ = mix([own_lse[4, 0, rows, :], incoming(0, i), incoming(1, i)])
        for side in range(2):
            link(side, i, 1).wait_recv()
        merged = jnp.concatenate(
            [
                own[4, 0, rows, t] * a
                + data_in[0, i, :, t].astype(F32) * b
                + data_in[1, i, :, t].astype(F32) * c
                for t in lane_tiles(LAT)
            ],
            axis=1,
        )
        upper = merged.astype(BF16)
        lower = (merged - upper.astype(F32)).astype(BF16)
        value = dot(upper, up_v[e]) + dot(lower, up_v[e])
        val_v[:, e * VDIM : (e + 1) * VDIM] = value.astype(BF16)


    def at_target(i):
        return at_z(ahead[i] * step, i % 2)

    for i in (3, 2, 1):
        remote(
            val_v, vals.at[i, core], z_send.at[1], z_recv.at[i, core], at_target(i)
        ).start()
    at_pair = remote(val_v, vals.at[0, core], z_send.at[0], z_recv.at[0, core], partner)

    @pl.when(core == 1)
    def _():
        at_pair.start()

    @pl.when(core == 0)
    def _():
        vals[0, 0] = val_v[...]

    def block_of(i):
        return lax.rem(z + step * i + NZ, NZ)

    swap_order = (block_of(core + 2) < block_of(core)).astype(jnp.int32)

    def distance(p):
        return core + 2 * (swap_order if p < 2 else 1 - swap_order)

    def await_half(i, h):
        remote(val_v, vals.at[i, h], z_send.at[0], z_recv.at[i, h], partner).wait_recv()

    for m in range(2):
        w_copy(m, 1 - core).wait_recv()

    def cross(p, k):
        return remote(
            x_out.at[p, k], x_in.at[p, k], x_send.at[p], x_recv.at[p], at_x(k + 1)
        )

    def crossed(p):
        return remote(x_out.at[p], x_in.at[p], x_send.at[p], x_recv.at[p], partner)

    def produce(p):
        i, m = distance(p), p % 2
        if m == 0:

            @pl.when(i != 0)
            def _():
                await_half(i, 0)

            await_half(i, 1)
        terms = dot(vals[i, 0], w_all[m, 0]) + dot(vals[i, 1], w_all[m, 1])
        for k, t in enumerate(lane_tiles(8 * LANES)):
            x_f[p, k] = terms[:, t]
        for k in (0, 2, 1):
            to = lax.rem(x + k + 1, NX)
            for c in range(2):
                x_out[p, k, c] = x_f[p, c * NX + to].astype(BF16)
            cross(p, k).start()

    def spread(p, c):
        column = twin if p % 2 else z
        to = {"ctx": y * 2 + c, "seq": block_of(distance(p))}
        return remote(
            z_out.at[p, c], z_in.at[column], a_send.at[p, c], a_recv.at[column], to
        )

    def consume(p):
        crossed(p).wait_recv()
        for c in range(2):
            total = x_f[p, c * NX + x]
            for k in range(3):
                total = total + x_in[p, k, c].astype(F32)
            z_out[p, c] = total.astype(BF16)
            if c == 0:

                @pl.when(distance(p) == 0)
                def _():
                    z_in[twin if p % 2 else z] = z_out[p, 0]

                @pl.when(distance(p) != 0)
                def _():
                    spread(p, 0).start()

            else:
                spread(p, c).start()

    for p in range(4):
        if p >= 2:
            crossed(p - 2).wait_send()
        if p == 3:
            consume(0)
        produce(p)
    for p in range(1, 4):
        consume(p)

    def last(k):
        to = lax.rem(y + k, NY)
        return remote(z_in.at[to], y_in.at[k], y_send, y_recv, at_y(k))

    for block in range(NZ):

        @pl.when(((block != z) & (block != twin)) | (core == 1))
        def _():
            remote(
                z_out.at[0, 0], z_in.at[block], a_send.at[0, 0], a_recv.at[block], partner
            ).wait_recv()

        k = lax.rem(block - y + NY, NY)

        @pl.when(k != 0)
        def _():
            last(k).start()

    others = y_in.at[1:NY]
    remote(others, others, y_send, y_recv, partner).wait_recv()
    total = z_in[y].astype(F32)
    for k in (1, 7, 2, 6, 3, 5, 4):
        total = total + y_in[k].astype(F32)
    out_ref[...] = total[:, :BLOCK].astype(BF16)

    remote(pair_in, pair_in, pair_send, pair_recv.at[0], partner).wait_send()
    for side in range(2):
        for k, buffer in enumerate((stat_out, data_out)):
            sent = buffer.at[side]
            remote(sent, sent, ring_send.at[side, k], ring_recv.at[side, 0, k], partner).wait_send()
    w_twin.wait_send()
    for m in range(2):
        w_copy(m, core).wait_send()
    three = vals.at[1:4, 0]
    remote(three, three, z_send.at[1], z_recv.at[0, 0], partner).wait_send()

    @pl.when(core == 1)
    def _():
        at_pair.wait_send()

    for p in range(4):
        if p >= 2:
            crossed(p).wait_send()
        spread(p, 1).wait_send()

        @pl.when(distance(p) != 0)
        def _():
            spread(p, 0).wait_send()

    remote(others, others, y_send, y_recv, partner).wait_send()


def shards(queries, latent_cache, selected, counts, value_up, output_proj_weight):
    rows, heads, width = queries.shape
    tokens = latent_cache.shape[0]
    weight = output_proj_weight[0].reshape(2 * VDIM, output_proj_weight.shape[3])
    hbm = pl.BlockSpec(memory_space=pl.ANY)
    vmem, dma = pltpu.VMEM, pltpu.SemaphoreType.DMA
    return pl.pallas_call(
        kernel,
        out_shape=jax.ShapeDtypeStruct((rows, BLOCK), BF16),
        in_specs=[hbm] * 6,
        out_specs=pl.BlockSpec(memory_space=pltpu.VMEM),
        scratch_shapes=[
            vmem(selected.shape, jnp.int32),
            vmem((1, rows), jnp.int32),
            vmem((2, rows, 16, width), BF16),
            vmem((width, tokens), BF16),
            vmem((2, LAT, VDIM), BF16),
            vmem((2,) + weight.shape, BF16),
            dma((7,)),
            vmem((64, LANES), F32),
            vmem((rows, tokens), F32),
            vmem((tokens, LAT), BF16),
            vmem((heads, rows, width), BF16),
            vmem((2, 256, tokens), F32),
            vmem((2, 256, tokens), BF16),
            vmem((2, 256, LANES), F32),
            vmem((8, 4, rows, LAT + LANES), F32),
            vmem((8, 2, rows, LAT + LANES), F32),
            dma,
            dma((8,)),
            vmem((5, 2, 2 * rows, LAT), F32),
            vmem((5, 2, 2 * rows, LANES), F32),
            vmem((2, 7, rows, LAT), BF16),
            vmem((2, 7, rows, LAT), BF16),
            vmem((2, 7, 8, LANES), F32),
            vmem((2, 7, 8, LANES), F32),
            dma((2, 2)),
            dma((2, 7, 2)),
            vmem((rows, 2 * VDIM), BF16),
            vmem((4, 2, rows, 2 * VDIM), BF16),
            vmem((2, 2, 2 * VDIM, 8 * LANES), BF16),
            dma((2,)),
            dma((2,)),
            dma,
            dma,
            dma((2,)),
            dma((4, 2)),
            vmem((4, 8, rows, LANES), F32),
            vmem((4, 3, 2, rows, LANES), BF16),
            vmem((4, 3, 2, rows, LANES), BF16),
            dma((4,)),
            dma((4,)),
            vmem((4, 2, rows, LANES), BF16),
            vmem((NZ, rows, LANES), BF16),
            dma((4, 2)),
            dma((NZ,)),
            vmem((NY, rows, LANES), BF16),
            dma,
            dma,
        ],
        compiler_params=pltpu.CompilerParams(
            collective_id=0, has_side_effects=True, vmem_limit_bytes=60 * 1024 * 1024
        ),
    )(selected, counts.T, queries, latent_cache.T, value_up[0], weight)


def solution(mesh):
    in_specs = (
        P("seq", "head", None),
        P("ctx", None),
        P("seq", "ctx", None),
        P("seq", "ctx"),
        P("head", "ctx", None, None),
        P("head", "ctx", None, "seq"),
    )
    out_specs = P("seq", ("ctx", "head"))
    return jax.shard_map(shards, mesh=mesh, in_specs=in_specs, out_specs=out_specs, check_vma=False)
```
